32 devices in a mesh: groups: 2 (over y), tensor: 4 (over z), dp: 4 (over x, core).
Axes of the slice: x: 2, y: 2, z: 4, core: 2. Of those that a mesh axis runs over, the one named last changes fastest.
Arguments:
- acts: bfloat16 [8, 288, 4096], P(('groups', 'dp')), parts along dimension 0, may hold values from -6 to 6
- out_grads: bfloat16 [8, 288, 14336], P(('groups', 'dp'), None, 'tensor'), parts along dimension 0, may hold values from -0.29882812 to 0.29882812
- basis_in: bfloat16 [8192, 4096], P(('groups', 'dp'), 'tensor'), parts along dimension 0, may hold values from -0.09375 to 0.09375
- basis_out: bfloat16 [28672, 14336], P(('groups', 'dp'), 'tensor'), parts along dimension 0, may hold values from -0.046875 to 0.046875
- lengths: int32 [8], P(('groups', 'dp')), parts along dimension 0, may hold values from 96 to 288
Outputs:
- corrections: bfloat16 [28672, 4096], P(('groups', 'tensor'), 'dp'), parts along dimension 0
The draws below stay inside these ranges and needn't reach their ends.
There are 2 independent parts, one for each index of `groups`. The reference program is written for one: setup_inputs(seed, part) draws one part's arguments, and reference() takes and returns one part's arrays. A program takes and returns all parts, laid end to end along the dimension named above; each array names one. Nothing has to cross between parts.
All inputs are finite; a program needn't handle non-finite values.
Results may differ from the reference program's by a relative error of at most 0.0085.
Values may be sent and summed in bfloat16 or wider, within the bound.
No kernel may reach another device: no remote copies, remote signals or barrier semaphores. Data moves between devices by JAX's collectives and lax.ppermute only.
A program may use at most 320 MiB of HBM per device.

```python
import jax
import jax.numpy as jnp
from jax import lax

D = 4096
FF = 14336
SEQ = 288
EX_DEV = 1
EXAMPLES = 4
N_DP = 4


def touch_ends(drawn, own_key, low, high):
    longest = drawn.shape.index(max(drawn.shape))
    spots = []
    for shift in (0, 1):
        where = [jax.random.randint(jax.random.fold_in(own_key, axis), (), 0, length) for axis, length in enumerate(drawn.shape)]
        where[longest] = (where[longest] + shift) % drawn.shape[longest]
        spots.append(tuple(where))
    return drawn.at[spots[0]].set(low).at[spots[1]].set(high)


def steps_of(key, shape, shards, low, largest):
    def one(axis_at, shards_of):
        steps = jax.random.uniform(jax.random.fold_in(jax.random.fold_in(key, 6), axis_at), (shards_of,), jnp.float32, low / len(shards), largest / len(shards))
        return jnp.repeat(jnp.exp(steps), shape[axis_at] // shards_of).reshape((-1,) + (1,) * (len(shape) - axis_at - 1))

    level = one(*shards[0])
    for cut in shards[1:]:
        level = level * one(*cut)
    return level


def noise(rng, extent, width, reach, shards=(), kind=jnp.bfloat16):
    values = jax.random.normal(rng, extent, jnp.float32) * width
    if len(shards) > 0:
        values = steps_of(rng, extent, shards, -0.22, 0.18) * values
    return jnp.clip(values, min=-reach, max=reach).astype(kind)


def setup_inputs(seed: int = 0, part: int = 0) -> dict:
    seeds = jax.random.split(jax.random.key(seed), 6)
    part_splits = jax.random.split(jax.random.fold_in(seeds[5], part), 6)
    return {
        "acts": noise(part_splits[0], (EXAMPLES, SEQ, D), 1.0, 6.0, ((0, 4),)),
        "out_grads": noise(part_splits[1], (EXAMPLES, SEQ, FF), 0.05, 0.29882812, ((0, 4), (2, 4))),
        "basis_in": noise(part_splits[2], (D, D), D ** -0.5, 0.09375, ((0, 4), (1, 4))),
        "basis_out": noise(part_splits[3], (FF, FF), FF ** -0.5, 0.046875, ((0, 4), (1, 4))),
        "lengths": touch_ends(jax.random.randint(part_splits[4], (EXAMPLES,), 96, SEQ + 1), jax.random.fold_in(part_splits[4], 1), 96, SEQ).astype(jnp.int32),
    }


def reference(acts, out_grads, basis_in, basis_out, lengths):
    acts_grp = acts.reshape(N_DP, EX_DEV, SEQ, D)
    grads_grp = out_grads.reshape(N_DP, EX_DEV, SEQ, FF)
    lens_grp = lengths.reshape(N_DP, EX_DEV)

    def group_term(inputs):
        acts_part, grads_part, lens_part = inputs

        def one_example(total, item):
            act_one, grad_one, len_one = item
            keep = (jnp.arange(SEQ, dtype=jnp.int32) < len_one).astype(acts.dtype)
            kept = act_one * keep[:, None]
            in_proj = jnp.dot(kept, basis_in, preferred_element_type=jnp.float32).astype(jnp.bfloat16)
            out_proj = jnp.dot(grad_one, basis_out, preferred_element_type=jnp.float32).astype(jnp.bfloat16)
            proj = jnp.dot(out_proj.T, in_proj, preferred_element_type=jnp.float32)
            return total + proj * proj, None

        start = jnp.zeros((FF, D), jnp.float32)
        total, _ = lax.scan(one_example, start, (acts_part, grads_part, lens_part))
        return total.astype(jnp.bfloat16)

    terms = lax.map(group_term, (acts_grp, grads_grp, lens_grp))
    return jnp.sum(terms.astype(jnp.float32), axis=0).astype(jnp.bfloat16)
```

```python
import jax
import jax.numpy as jnp
from jax import lax
from jax.experimental import pallas as pl
from jax.experimental.pallas import tpu as pltpu
from jax.sharding import PartitionSpec as P

F32 = jnp.float32
BF16 = jnp.bfloat16


def square_kernel(out_ref, in_ref, c_ref):
    total = None
    for n in range(out_ref.shape[0]):
        proj = lax.dot_general(out_ref[n], in_ref[n], (((0,), (0,)), ((), ())), preferred_element_type=F32)
        total = proj * proj if total is None else total + proj * proj
    c_ref[...] = total.astype(c_ref.dtype)


def squares(out_proj, in_proj):
    n, seq, cols = out_proj.shape
    ins = in_proj.shape[2]
    tile = cols
    for t in (512, 256, 128):
        if cols % t == 0:
            tile = t
            break
    return pl.pallas_call(
        square_kernel,
        grid=(cols // tile,),
        in_specs=[
            pl.BlockSpec((n, seq, tile), lambda i: (0, 0, i)),
            pl.BlockSpec((n, seq, ins), lambda i: (0, 0, 0)),
        ],
        out_specs=pl.BlockSpec((tile, ins), lambda i: (i, 0)),
        out_shape=jax.ShapeDtypeStruct((cols, ins), BF16),
        compiler_params=pltpu.CompilerParams(vmem_limit_bytes=48 * 2**20),
        cost_estimate=pl.CostEstimate(
            flops=2 * n * seq * cols * ins, bytes_accessed=2 * (n * seq * (cols + ins) + cols * ins), transcendentals=0
        ),
    )(out_proj, in_proj)


def make(n_dp):
    def swap(x, k):
        return lax.ppermute(x, "dp", [(d, d ^ k) for d in range(n_dp)])

    def per_device(acts, out_grads, basis_in, basis_out, lengths):
        seq = acts.shape[1]
        me = lax.axis_index("dp")
        keep = (jnp.arange(seq, dtype=jnp.int32)[None, :] < lengths[:, None]).astype(acts.dtype)
        kept = (acts * keep[:, :, None])[0]

        def exchange(x, width):
            parts = [lax.dynamic_slice_in_dim(x, (me ^ k) * width, width, axis=1) for k in range(n_dp)]
            return [parts[0]] + [swap(parts[k], k) for k in range(1, n_dp)]

        rows = basis_in.shape[0]
        b0 = basis_in
        b2 = swap(b0, 2)
        b1 = swap(b0, 1)
        b3 = swap(b2, 1)
        blocks = [b0, b1, b2, b3]
        in_local = None
        for k in range(n_dp):
            a = lax.dynamic_slice_in_dim(kept, (me ^ k) * rows, rows, axis=1)
            t = jnp.dot(a, blocks[k], preferred_element_type=F32)
            in_local = t if in_local is None else in_local + t
        in_local = in_local.astype(BF16)

        n_chunks = 3
        step = seq // n_chunks
        wide = out_grads.shape[2] * lax.axis_size("tensor") // n_dp
        outs = []
        in_proj = None
        for j in range(n_chunks):
            g = out_grads[0, j * step : (j + 1) * step]
            whole = lax.all_gather(g, "tensor", axis=1, tiled=True)
            mine = exchange(whole, wide)
            part = [jnp.dot(m, basis_out, preferred_element_type=F32) for m in mine]
            odd = swap(jnp.stack([part[1], part[3]]).astype(BF16), 1)
            s0 = part[0] + odd[0].astype(F32)
            s2 = part[2] + odd[1].astype(F32)
            far = swap(jnp.stack([s2, s0]).astype(BF16), 2)
            even = jnp.stack([(s0 + far[0].astype(F32)).astype(BF16), (s2 + far[1].astype(F32)).astype(BF16)])
            rest = swap(even, 1)
            outs.append(jnp.stack([even[0], rest[0], even[1], rest[1]]))
        in_all = lax.all_gather(in_local, "tensor", axis=1, tiled=True)
        in_proj = jnp.stack(exchange(in_all, in_all.shape[1] // n_dp))
        out_proj = jnp.concatenate(outs, axis=1)
        return squares(out_proj, in_proj)

    return per_device


def solution(mesh):
    in_specs = (
        P(("groups", "dp"), None, None),
        P(("groups", "dp"), None, "tensor"),
        P(("groups", "dp"), "tensor"),
        P(("groups", "dp"), "tensor"),
        P(("groups", "dp")),
    )
    out_specs = P(("groups", "tensor"), "dp")
    return jax.shard_map(
        make(mesh.shape["dp"]), mesh=mesh, in_specs=in_specs, out_specs=out_specs, check_vma=False
    )
```

```python
import functools

import jax
import jax.numpy as jnp
from jax import lax
from jax.experimental import pallas as pl
from jax.experimental.pallas import tpu as pltpu
from jax.sharding import PartitionSpec as P

F32 = jnp.float32
BF16 = jnp.bfloat16
MIN_LEN = 96
ALIGN = 16
STEPS = 6


def square_kernel(start_ref, out_ref, in_ref, c_ref):
    total = None
    for n in range(in_ref.shape[0]):
        rows = pl.ds(pl.multiple_of(start_ref[n], ALIGN), in_ref.shape[1])
        proj = lax.dot_general(out_ref[rows, :], in_ref[n], (((0,), (0,)), ((), ())), preferred_element_type=F32)
        total = proj * proj if total is None else total + proj * proj
    c_ref[...] = total.astype(c_ref.dtype)


def squares(starts, out_proj, in_proj):
    tokens, cols = out_proj.shape
    n, seq, ins = in_proj.shape
    tile = cols
    for t in (512, 256, 128):
        if cols % t == 0:
            tile = t
            break
    return pl.pallas_call(
        square_kernel,
        grid_spec=pltpu.PrefetchScalarGridSpec(
            num_scalar_prefetch=1,
            grid=(cols // tile,),
            in_specs=[
                pl.BlockSpec((tokens, tile), lambda i, s: (0, i)),
                pl.BlockSpec((n, seq, ins), lambda i, s: (0, 0, 0)),
            ],
            out_specs=pl.BlockSpec((tile, ins), lambda i, s: (i, 0)),
        ),
        out_shape=jax.ShapeDtypeStruct((cols, ins), BF16),
        compiler_params=pltpu.CompilerParams(vmem_limit_bytes=48 * 2**20),
        cost_estimate=pl.CostEstimate(
            flops=2 * n * seq * cols * ins, bytes_accessed=2 * (n * seq * (cols + ins) + cols * ins), transcendentals=0
        ),
    )(starts, out_proj, in_proj)


def swap_dp(x, k, n_dp):
    return lax.ppermute(x, "dp", [(d, d ^ k) for d in range(n_dp)])


def project_in(kept, basis_in, me, n_dp):
    rows = basis_in.shape[0]
    b0 = basis_in
    b2 = swap_dp(b0, 2, n_dp)
    b1 = swap_dp(b0, 1, n_dp)
    b3 = swap_dp(b2, 1, n_dp)
    total = None
    for k, b in enumerate([b0, b1, b2, b3]):
        a = lax.dynamic_slice_in_dim(kept, (me ^ k) * rows, rows, axis=1)
        t = jnp.dot(a, b, preferred_element_type=F32)
        total = t if total is None else total + t
    return total.astype(BF16)


def mask_acts(acts, lengths):
    keep = (jnp.arange(acts.shape[1], dtype=jnp.int32)[None, :] < lengths[:, None]).astype(acts.dtype)
    return (acts * keep[:, :, None])[0]


def general(n_dp, acts, out_grads, basis_in, basis_out, lengths):
    seq = acts.shape[1]
    me = lax.axis_index("dp")
    kept = mask_acts(acts, lengths)

    def exchange(x, width):
        parts = [lax.dynamic_slice_in_dim(x, (me ^ k) * width, width, axis=1) for k in range(n_dp)]
        return [parts[0]] + [swap_dp(parts[k], k, n_dp) for k in range(1, n_dp)]

    in_local = project_in(kept, basis_in, me, n_dp)
    n_chunks = 3
    step = seq // n_chunks
    outs = []
    for j in range(n_chunks):
        g = out_grads[0, j * step : (j + 1) * step]
        whole = lax.all_gather(g, "tensor", axis=1, tiled=True)
        mine = jnp.concatenate(exchange(whole, whole.shape[1] // n_dp), axis=0)
        part = jnp.dot(mine, basis_out, preferred_element_type=F32)
        part = part.reshape(n_dp, step, -1)
        odd = swap_dp(part[1::2].astype(BF16), 1, n_dp)
        s0 = part[0] + odd[0].astype(F32)
        s2 = part[2] + odd[1].astype(F32)
        far = swap_dp(jnp.stack([s2, s0]).astype(BF16), 2, n_dp)
        even = jnp.stack([s0 + far[0].astype(F32), s2 + far[1].astype(F32)]).astype(BF16)
        rest = swap_dp(even, 1, n_dp)
        outs.append(jnp.stack([even[0], rest[0], even[1], rest[1]]))
    in_all = lax.all_gather(in_local, "tensor", axis=1, tiled=True)
    in_proj = jnp.stack(exchange(in_all, in_all.shape[1] // n_dp))
    out_proj = jnp.concatenate(outs, axis=1).reshape(n_dp * seq, -1)
    return squares(jnp.arange(n_dp, dtype=jnp.int32) * seq, out_proj, in_proj)


def home_pairs(hops, across=False):
    pairs = []
    for x in (0, 1):
        for c in (0, 1):
            d = 2 * x + c
            for w0, w1 in hops:
                z0, z1 = (w0, w1) if x == 0 else (3 - w0, 3 - w1)
                if across:
                    pairs.append((z0 * 4 + (d ^ 2), z1 * 4 + d))
                else:
                    pairs.append((z0 * 4 + d, z1 * 4 + d))
    return pairs


def send(x, hops, across=False):
    return lax.ppermute(x, ("tensor", "dp"), home_pairs(hops, across))


def to_home(x):
    return send(x, [(0, 0), (1, 1)], True)


def chain(own, w):
    r1 = send(own, [(0, 1), (1, 2)])
    m1 = send(own, [(1, 0)])
    r2 = send(r1, [(1, 2), (2, 3)])
    r3 = send(r2, [(2, 3)])
    outer = jnp.where(w == 0, own, jnp.where(w == 1, r1, jnp.where(w == 2, r2, r3)))
    inner = jnp.where(w == 0, m1, jnp.where(w == 1, own, jnp.where(w == 2, r1, r2)))
    return outer, inner


def compact(cap, kept, grads, basis_in, basis_out, lens):
    seq = kept.shape[0]
    me = lax.axis_index("dp")
    z = lax.axis_index("tensor")
    x, c = me // 2, me % 2
    w = jnp.where(x == 0, z, 3 - z)
    m = STEPS
    u = cap // m
    c2 = min(m, -(-min(2 * seq, cap - 2 * MIN_LEN) // u))
    half = grads.shape[1]

    al = (lens + ALIGN - 1) // ALIGN * ALIGN
    off = jnp.stack([jnp.int32(0), al[0], cap - al[3] - al[2], cap - al[3]])

    pos = jnp.arange(c2 * u, dtype=jnp.int32)
    chunk = pos // u
    row = jnp.where(x == 0, chunk, m - 1 - chunk) * u + pos % u
    s = jnp.arange(seq, dtype=jnp.int32)

    def pick(n):
        return (row[:, None] == (off[n] + s)[None, :]) & (s < lens[n])[None, :]

    hot = jnp.concatenate([pick(me), pick(me ^ 1)], axis=1).astype(BF16)

    def pack(v):
        return jnp.dot(hot, v, preferred_element_type=F32).astype(BF16).reshape(c2, u, v.shape[1])

    def swap(v, k=1):
        return swap_dp(v, k, 4)

    packed = pack(grads)
    cut = max(1, c2 // 2)
    arrived = [None] * c2
    for lo, hi in ((cut, c2), (0, cut)):
        if hi > lo:
            got = to_home(packed[lo:hi])
            for i in range(lo, hi):
                arrived[i] = got[i - lo]

    def merged(own, others, i):
        t = None
        if i < c2:
            t = own[i]
        if m - 1 - i < c2:
            o = others[m - 1 - i]
            t = o if t is None else t + o
        return t

    want_outer = c == x
    sums, fars = [], []
    for i in range(m):
        outer, inner = chain(merged(packed, arrived, i), w)
        mine = jnp.where(want_outer, outer, inner)
        other = swap(jnp.where(want_outer, inner, outer))
        g = jnp.where(c == 0, jnp.concatenate([mine, other], 1), jnp.concatenate([other, mine], 1))
        part = jnp.dot(g, basis_out, preferred_element_type=F32)
        cols = part.shape[1] // 2
        given = lax.dynamic_slice_in_dim(part, (1 - c) * cols, cols, axis=1).astype(BF16)
        held = lax.dynamic_slice_in_dim(part, c * cols, cols, axis=1)
        held = held + swap(given).astype(F32)
        sums.append(held)
        fars.append(swap(held.astype(BF16), 2))

    in_local = project_in(kept, basis_in, me, 4)
    hc = in_local.shape[1] // 2
    in_mine = lax.dynamic_slice_in_dim(in_local, c * hc, hc, axis=1)
    in_given = lax.dynamic_slice_in_dim(in_local, (1 - c) * hc, hc, axis=1)
    in_packed = pack(jnp.concatenate([in_mine, swap(in_given)], axis=0))
    in_arrived = to_home(in_packed)
    in_t = jnp.concatenate([merged(in_packed, in_arrived, i) for i in range(m)], axis=0)
    outer, inner = chain(in_t, w)
    mine = jnp.where(want_outer, outer, inner)
    other = swap(jnp.where(want_outer, inner, outer))
    in_t = jnp.where(c == 0, jnp.concatenate([mine, other], 1), jnp.concatenate([other, mine], 1))
    in_t = in_t.reshape(m, u, 2 * hc)
    in_t = jnp.where(x == 0, in_t, in_t[::-1]).reshape(cap, 2 * hc)

    nat = [None] * m
    for j in range(m // 2 - 1, -1, -1):
        k = m - 1 - j
        lo = jnp.where(x == 0, sums[j], sums[k]) + jnp.where(x == 0, fars[k], fars[j]).astype(F32)
        hi = jnp.where(x == 0, sums[k], sums[j]) + jnp.where(x == 0, fars[j], fars[k]).astype(F32)
        two = jnp.stack([lo, hi]).astype(BF16)
        rest = swap(two)
        both = jnp.where(c == 0, jnp.concatenate([two, rest], 2), jnp.concatenate([rest, two], 2))
        nat[j], nat[k] = both[0], both[1]
    out_t = jnp.concatenate(nat, axis=0)

    ends = off + al
    starts = jnp.stack([off[0], off[1], ends[2] - seq, ends[3] - seq]).astype(jnp.int32)
    wins = []
    for n in range(4):
        rows = starts[n] + s
        mine = (rows >= off[n]) & (rows < off[n] + lens[n])
        win = lax.dynamic_slice_in_dim(in_t, starts[n], seq, axis=0)
        wins.append(jnp.where(mine[:, None], win, jnp.zeros_like(win)))
    return squares(starts, out_t, jnp.stack(wins))


def special(caps, acts, out_grads, basis_in, basis_out, lengths):
    me = lax.axis_index("dp")
    c = me % 2
    every = lax.all_gather(lengths, ("groups", "dp"), axis=0, tiled=True)
    kept = mask_acts(acts, lengths)
    g = out_grads[0]
    half = g.shape[1] // 2
    mine = lax.dynamic_slice_in_dim(g, c * half, half, axis=1)
    given = lax.dynamic_slice_in_dim(g, (1 - c) * half, half, axis=1)
    grads = jnp.concatenate([mine, swap_dp(given, 1, 4)], axis=0)
    totals = jnp.sum(((every + ALIGN - 1) // ALIGN * ALIGN).reshape(-1, 4), axis=1)
    need = jnp.max(totals)
    lens = lax.dynamic_slice_in_dim(every, lax.axis_index("groups") * 4, 4)
    index = jnp.int32(0)
    for cap in caps[:-1]:
        index = index + (need > cap).astype(jnp.int32)
    branches = [functools.partial(compact, cap) for cap in caps]
    return lax.switch(index, branches, kept, grads, basis_in, basis_out, lens)


def per_device(sizes, caps, acts, out_grads, basis_in, basis_out, lengths):
    if sizes == (4, 4):
        return special(caps, acts, out_grads, basis_in, basis_out, lengths)
    return general(sizes[1], acts, out_grads, basis_in, basis_out, lengths)


CAPS = (768, 960, 1152)


def solution(mesh):
    in_specs = (
        P(("groups", "dp"), None, None),
        P(("groups", "dp"), None, "tensor"),
        P(("groups", "dp"), "tensor"),
        P(("groups", "dp"), "tensor"),
        P(("groups", "dp")),
    )
    out_specs = P(("groups", "tensor"), "dp")
    sizes = (mesh.shape["tensor"], mesh.shape["dp"])
    return jax.shard_map(
        functools.partial(per_device, sizes, CAPS), mesh=mesh, in_specs=in_specs, out_specs=out_specs, check_vma=False
    )
```

```python
import functools

import jax
import jax.numpy as jnp
from jax import lax
from jax.experimental import pallas as pl
from jax.experimental.pallas import tpu as pltpu
from jax.sharding import PartitionSpec as P

F32 = jnp.float32
BF16 = jnp.bfloat16
MIN_LEN = 96
ALIGN = 16
STEPS = 4


def square_kernel(start_ref, out_ref, in_ref, c_ref):
    total = None
    for n in range(in_ref.shape[0]):
        rows = pl.ds(pl.multiple_of(start_ref[n], ALIGN), in_ref.shape[1])
        proj = lax.dot_general(out_ref[rows, :], in_ref[n], (((0,), (0,)), ((), ())), preferred_element_type=F32)
        total = proj * proj if total is None else total + proj * proj
    c_ref[...] = total.astype(c_ref.dtype)


def squares(starts, out_proj, in_proj):
    tokens, cols = out_proj.shape
    n, seq, ins = in_proj.shape
    tile = cols
    for t in (512, 256, 128):
        if cols % t == 0:
            tile = t
            break
    return pl.pallas_call(
        square_kernel,
        grid_spec=pltpu.PrefetchScalarGridSpec(
            num_scalar_prefetch=1,
            grid=(cols // tile,),
            in_specs=[
                pl.BlockSpec((tokens, tile), lambda i, s: (0, i)),
                pl.BlockSpec((n, seq, ins), lambda i, s: (0, 0, 0)),
            ],
            out_specs=pl.BlockSpec((tile, ins), lambda i, s: (i, 0)),
        ),
        out_shape=jax.ShapeDtypeStruct((cols, ins), BF16),
        compiler_params=pltpu.CompilerParams(vmem_limit_bytes=60 * 2**20),
        cost_estimate=pl.CostEstimate(
            flops=2 * n * seq * cols * ins, bytes_accessed=2 * (n * seq * (cols + ins) + cols * ins), transcendentals=0
        ),
    )(starts, out_proj, in_proj)


def swap_dp(x, k, n_dp):
    return lax.ppermute(x, "dp", [(d, d ^ k) for d in range(n_dp)])


def project_in(kept, basis_in, far_in, me, n_dp=4):
    rows = basis_in.shape[0]
    near = swap_dp(basis_in, 1, n_dp)
    far_near = swap_dp(far_in, 1, n_dp)
    total = None
    for k, b in enumerate([basis_in, near, far_in, far_near]):
        a = lax.dynamic_slice_in_dim(kept, (me ^ k) * rows, rows, axis=1)
        t = jnp.dot(a, b, preferred_element_type=F32)
        total = t if total is None else total + t
    return total.astype(BF16)


def mask_acts(acts, lengths):
    keep = (jnp.arange(acts.shape[1], dtype=jnp.int32)[None, :] < lengths[:, None]).astype(acts.dtype)
    return (acts * keep[:, :, None])[0]


def general(n_dp, acts, out_grads, basis_in, basis_out, lengths):
    seq = acts.shape[1]
    me = lax.axis_index("dp")
    kept = mask_acts(acts, lengths)

    def exchange(x, width):
        parts = [lax.dynamic_slice_in_dim(x, (me ^ k) * width, width, axis=1) for k in range(n_dp)]
        return [parts[0]] + [swap_dp(parts[k], k, n_dp) for k in range(1, n_dp)]

    in_local = project_in(kept, basis_in, swap_dp(basis_in, 2, n_dp), me, n_dp)
    n_chunks = 3
    step = seq // n_chunks
    outs = []
    for j in range(n_chunks):
        g = out_grads[0, j * step : (j + 1) * step]
        whole = lax.all_gather(g, "tensor", axis=1, tiled=True)
        mine = jnp.concatenate(exchange(whole, whole.shape[1] // n_dp), axis=0)
        part = jnp.dot(mine, basis_out, preferred_element_type=F32)
        part = part.reshape(n_dp, step, -1)
        odd = swap_dp(part[1::2].astype(BF16), 1, n_dp)
        s0 = part[0] + odd[0].astype(F32)
        s2 = part[2] + odd[1].astype(F32)
        far = swap_dp(jnp.stack([s2, s0]).astype(BF16), 2, n_dp)
        even = jnp.stack([s0 + far[0].astype(F32), s2 + far[1].astype(F32)]).astype(BF16)
        rest = swap_dp(even, 1, n_dp)
        outs.append(jnp.stack([even[0], rest[0], even[1], rest[1]]))
    in_all = lax.all_gather(in_local, "tensor", axis=1, tiled=True)
    in_proj = jnp.stack(exchange(in_all, in_all.shape[1] // n_dp))
    out_proj = jnp.concatenate(outs, axis=1).reshape(n_dp * seq, -1)
    return squares(jnp.arange(n_dp, dtype=jnp.int32) * seq, out_proj, in_proj)


def home_pairs(hops, across=False):
    pairs = []
    for x in (0, 1):
        for c in (0, 1):
            d = 2 * x + c
            for w0, w1 in hops:
                z0, z1 = (w0, w1) if x == 0 else (3 - w0, 3 - w1)
                if across:
                    pairs.append((z0 * 4 + (d ^ 2), z1 * 4 + d))
                else:
                    pairs.append((z0 * 4 + d, z1 * 4 + d))
    return pairs


def send(x, hops, across=False):
    return lax.ppermute(x, ("tensor", "dp"), home_pairs(hops, across))


def to_home(x):
    return send(x, [(0, 0), (1, 1)], True)


def tie(v, *after):
    return lax.optimization_barrier((v,) + after)[0]


def swap(v, k=1):
    return swap_dp(v, k, 4)


def compact(cap, kept, grads, basis_in, far_in, basis_out, lens):
    seq = kept.shape[0]
    me = lax.axis_index("dp")
    z = lax.axis_index("tensor")
    x, c = me // 2, me % 2
    w = jnp.where(x == 0, z, 3 - z)
    m = STEPS
    u = cap // m
    c2 = min(m, -(-min(2 * seq, cap - 2 * MIN_LEN) // u))
    want_outer = c == x

    al = (lens + ALIGN - 1) // ALIGN * ALIGN
    off = jnp.stack([jnp.int32(0), al[0], cap - al[3] - al[2], cap - al[3]])

    pos = jnp.arange(c2 * u, dtype=jnp.int32)
    chunk = pos // u
    row = jnp.where(x == 0, chunk, m - 1 - chunk) * u + pos % u
    s = jnp.arange(seq, dtype=jnp.int32)

    def pick(n):
        return (row[:, None] == (off[n] + s)[None, :]) & (s < lens[n])[None, :]

    hot = jnp.concatenate([pick(me), pick(me ^ 1)], axis=1).astype(BF16)

    def pack(v):
        return jnp.dot(hot, v, preferred_element_type=F32).astype(BF16).reshape(c2, u, v.shape[1])

    def merged(own, others, i):
        t = None
        if i < c2:
            t = own[i]
        if m - 1 - i < c2:
            o = others[m - 1 - i]
            t = o if t is None else t + o
        return t

    def whole(outer, inner, *after):
        mine = jnp.where(want_outer, outer, inner)
        other = swap(tie(jnp.where(want_outer, inner, outer), *after))
        return jnp.where(c == 0, jnp.concatenate([mine, other], 1), jnp.concatenate([other, mine], 1))

    packed = pack(grads)
    arrived = [None] * c2
    last = None
    for i in range(c2 - 1, -1, -1):
        arrived[i] = to_home(packed[i] if last is None else tie(packed[i], last))
        if last is None:
            rest_in = swap(tie(basis_in[far_in.shape[0] :], arrived[i]), 2)
        last = arrived[i]
    far_in = jnp.concatenate([far_in, rest_in], axis=0)

    parts, sums, fars = [None] * m, [None] * m, [None] * m
    own, fa, fb, m1 = [None] * m, [None] * (m + 1), [None] * m, [None] * m

    def product(i):
        outer = jnp.where(w == 0, own[i], jnp.where(w == 1, fa[i], jnp.where(w == 2, fb[i], fa[i + 1])))
        inner = jnp.where(w == 0, m1[i], jnp.where(w == 1, own[i], jnp.where(w == 2, fa[i], fb[i])))
        parts[i] = jnp.dot(whole(outer, inner), basis_out, preferred_element_type=F32)

    def add_core(i):
        cols = parts[i].shape[1] // 2
        given = lax.dynamic_slice_in_dim(parts[i], (1 - c) * cols, cols, axis=1).astype(BF16)
        held = lax.dynamic_slice_in_dim(parts[i], c * cols, cols, axis=1)
        sums[i] = held + swap(given).astype(F32)
        fars[i] = swap(sums[i].astype(BF16), 2)

    in_own = None
    for i in range(m):
        own[i] = merged(packed, arrived, i)
        v = own[i] if i == 0 else jnp.where(w == 2, fb[i - 1], own[i])
        after = []
        if i >= 2:
            after.append(parts[i - 2])
        if i == m - 1:
            in_local = project_in(kept, basis_in, far_in, me)
            after.append(in_local)
        fa[i] = send(tie(v, *after), [(0, 1), (1, 2)] + ([(2, 3)] if i else []))
        m1[i] = send(own[i], [(1, 0)])
        if i >= 1:
            product(i - 1)
        if i >= 2:
            add_core(i - 2)
        after = []
        if i >= 2:
            after.append(sums[i - 2])
        if i >= 3:
            after.append(fars[i - 3])
        fb[i] = send(tie(fa[i], *after), [(1, 2), (2, 3)])

    hc = in_local.shape[1] // 2
    in_mine = lax.dynamic_slice_in_dim(in_local, c * hc, hc, axis=1)
    in_given = lax.dynamic_slice_in_dim(in_local, (1 - c) * hc, hc, axis=1)
    in_packed = pack(jnp.concatenate([in_mine, swap(in_given)], axis=0))
    in_arrived = to_home(in_packed)
    in_own = jnp.concatenate([merged(in_packed, in_arrived, i) for i in range(m)], axis=0)

    fa[m] = send(tie(fb[m - 1], parts[m - 2]), [(2, 3)])
    r1 = send(tie(in_own, fb[m - 1], parts[m - 2]), [(0, 1), (1, 2)])
    i1 = send(in_own, [(1, 0)])
    product(m - 1)
    add_core(m - 2)
    r2 = send(tie(r1, fa[m], sums[m - 2]), [(1, 2), (2, 3)])
    add_core(m - 1)
    r3 = send(tie(r2, parts[m - 1]), [(2, 3)])
    outer = jnp.where(w == 0, in_own, jnp.where(w == 1, r1, jnp.where(w == 2, r2, r3)))
    inner = jnp.where(w == 0, i1, jnp.where(w == 1, in_own, jnp.where(w == 2, r1, r2)))
    in_t = whole(outer, inner).reshape(m, u, 2 * hc)
    in_t = jnp.where(x == 0, in_t, in_t[::-1]).reshape(cap, 2 * hc)

    nat = [None] * m
    for j in range(m // 2 - 1, -1, -1):
        k = m - 1 - j
        lo = jnp.where(x == 0, sums[j], sums[k]) + jnp.where(x == 0, fars[k], fars[j]).astype(F32)
        hi = jnp.where(x == 0, sums[k], sums[j]) + jnp.where(x == 0, fars[j], fars[k]).astype(F32)
        two = jnp.stack([lo, hi]).astype(BF16)
        rest = swap(two)
        both = jnp.where(c == 0, jnp.concatenate([two, rest], 2), jnp.concatenate([rest, two], 2))
        nat[j], nat[k] = both[0], both[1]
    out_t = jnp.concatenate(nat, axis=0)

    ends = off + al
    starts = jnp.stack([off[0], off[1], ends[2] - seq, ends[3] - seq]).astype(jnp.int32)
    wins = []
    for n in range(4):
        rows = starts[n] + s
        mine = (rows >= off[n]) & (rows < off[n] + lens[n])
        win = lax.dynamic_slice_in_dim(in_t, starts[n], seq, axis=0)
        wins.append(jnp.where(mine[:, None], win, jnp.zeros_like(win)))
    return squares(starts, out_t, jnp.stack(wins))


def special(caps, acts, out_grads, basis_in, basis_out, lengths):
    me = lax.axis_index("dp")
    c = me % 2
    far_in = swap_dp(basis_in[: basis_in.shape[0] // 2], 2, 4)
    every = lax.all_gather(lengths, ("groups", "dp"), axis=0, tiled=True)
    kept = mask_acts(acts, lengths)
    g = out_grads[0]
    half = g.shape[1] // 2
    mine = lax.dynamic_slice_in_dim(g, c * half, half, axis=1)
    given = lax.dynamic_slice_in_dim(g, (1 - c) * half, half, axis=1)
    grads = jnp.concatenate([mine, swap_dp(given, 1, 4)], axis=0)
    totals = jnp.sum(((every + ALIGN - 1) // ALIGN * ALIGN).reshape(-1, 4), axis=1)
    need = jnp.max(totals)
    lens = lax.dynamic_slice_in_dim(every, lax.axis_index("groups") * 4, 4)
    index = jnp.int32(0)
    for cap in caps[:-1]:
        index = index + (need > cap).astype(jnp.int32)
    branches = [functools.partial(compact, cap) for cap in caps]
    return lax.switch(index, branches, kept, grads, basis_in, far_in, basis_out, lens)


def per_device(sizes, caps, acts, out_grads, basis_in, basis_out, lengths):
    if sizes == (4, 4):
        return special(caps, acts, out_grads, basis_in, basis_out, lengths)
    return general(sizes[1], acts, out_grads, basis_in, basis_out, lengths)


CAPS = (768, 832, 896, 960, 1152)


def solution(mesh):
    in_specs = (
        P(("groups", "dp"), None, None),
        P(("groups", "dp"), None, "tensor"),
        P(("groups", "dp"), "tensor"),
        P(("groups", "dp"), "tensor"),
        P(("groups", "dp")),
    )
    out_specs = P(("groups", "tensor"), "dp")
    sizes = (mesh.shape["tensor"], mesh.shape["dp"])
    return jax.shard_map(
        functools.partial(per_device, sizes, CAPS), mesh=mesh, in_specs=in_specs, out_specs=out_specs, check_vma=False
    )
```

```python
import functools

import jax
import jax.numpy as jnp
from jax import lax
from jax.experimental import pallas as pl
from jax.experimental.pallas import tpu as pltpu
from jax.sharding import PartitionSpec as P

F32 = jnp.float32
BF16 = jnp.bfloat16
MIN_LEN = 96
ALIGN = 16
TILE = 256
STEPS = 4


def square_kernel(start_ref, out_ref, in_ref, c_ref):
    total = None
    for n in range(in_ref.shape[0]):
        rows = pl.ds(pl.multiple_of(start_ref[n], ALIGN), in_ref.shape[1])
        proj = lax.dot_general(out_ref[rows, :], in_ref[n], (((0,), (0,)), ((), ())), preferred_element_type=F32)
        total = proj * proj if total is None else total + proj * proj
    c_ref[...] = total.astype(c_ref.dtype)


def squares(starts, out_proj, in_proj):
    tokens, cols = out_proj.shape
    n, seq, ins = in_proj.shape
    tile = cols
    for t in (512, 256, 128):
        if cols % t == 0:
            tile = t
            break
    return pl.pallas_call(
        square_kernel,
        grid_spec=pltpu.PrefetchScalarGridSpec(
            num_scalar_prefetch=1,
            grid=(cols // tile,),
            in_specs=[
                pl.BlockSpec((tokens, tile), lambda i, s: (0, i)),
                pl.BlockSpec((n, seq, ins), lambda i, s: (0, 0, 0)),
            ],
            out_specs=pl.BlockSpec((tile, ins), lambda i, s: (i, 0)),
        ),
        out_shape=jax.ShapeDtypeStruct((cols, ins), BF16),
        compiler_params=pltpu.CompilerParams(vmem_limit_bytes=60 * 2**20),
        cost_estimate=pl.CostEstimate(
            flops=2 * n * seq * cols * ins, bytes_accessed=2 * (n * seq * (cols + ins) + cols * ins), transcendentals=0
        ),
    )(starts, out_proj, in_proj)


def product_kernel(c_ref, mine_ref, other_ref, b_mine_ref, b_other_ref, given_ref, held_ref):
    i = pl.program_id(0)
    total = jnp.dot(mine_ref[...], b_mine_ref[...], preferred_element_type=F32)
    total = total + jnp.dot(other_ref[...], b_other_ref[...], preferred_element_type=F32)

    @pl.when(i < pl.num_programs(0) // 2)
    def _():
        given_ref[...] = total.astype(given_ref.dtype)

    @pl.when(i >= pl.num_programs(0) // 2)
    def _():
        held_ref[...] = total


def products(c, mine, other, basis):
    rows, depth = mine.shape
    cols = basis.shape[1] // 2
    tile = TILE
    per = cols // tile
    at = lambda i, c: jnp.where(i < per, (1 - c[0]) * per + i, c[0] * per + i - per)
    return pl.pallas_call(
        product_kernel,
        grid_spec=pltpu.PrefetchScalarGridSpec(
            num_scalar_prefetch=1,
            grid=(2 * per,),
            in_specs=[
                pl.BlockSpec((rows, depth), lambda i, c: (0, 0)),
                pl.BlockSpec((rows, depth), lambda i, c: (0, 0)),
                pl.BlockSpec((depth, tile), lambda i, c: (c[0], at(i, c))),
                pl.BlockSpec((depth, tile), lambda i, c: (1 - c[0], at(i, c))),
            ],
            out_specs=[
                pl.BlockSpec((rows, tile), lambda i, c: (0, jnp.minimum(i, per - 1))),
                pl.BlockSpec((rows, tile), lambda i, c: (0, jnp.maximum(i - per, 0))),
            ],
        ),
        out_shape=[jax.ShapeDtypeStruct((rows, cols), BF16), jax.ShapeDtypeStruct((rows, cols), F32)],
        compiler_params=pltpu.CompilerParams(vmem_limit_bytes=32 * 2**20),
        cost_estimate=pl.CostEstimate(
            flops=8 * rows * depth * cols,
            bytes_accessed=4 * rows * depth + 8 * depth * cols + 6 * rows * cols,
            transcendentals=0,
        ),
    )(c.reshape(1), mine, other, basis, basis)


def pieces_kernel(pairs, start_ref, c_ref, *refs):
    own, rest, in_ref, out_ref, held = refs[:pairs], refs[pairs : 2 * pairs], refs[-3], refs[-2], refs[-1]
    i = pl.program_id(0)
    u = own[0].shape[1]

    def fill(parts):
        for j, part in enumerate(parts):
            held[j * u : (j + 1) * u, :] = part[0]
            k = 2 * pairs - 1 - j
            held[k * u : (k + 1) * u, :] = part[1]

    @pl.when(i < pl.num_programs(0) // 2)
    def _():
        fill(own)

    @pl.when(i >= pl.num_programs(0) // 2)
    def _():
        fill(rest)

    total = None
    for n in range(in_ref.shape[0]):
        rows = pl.ds(pl.multiple_of(start_ref[n], ALIGN), in_ref.shape[1])
        proj = lax.dot_general(held[rows, :], in_ref[n], (((0,), (0,)), ((), ())), preferred_element_type=F32)
        total = proj * proj if total is None else total + proj * proj
    out_ref[...] = total.astype(out_ref.dtype)


def squares_of_pieces(starts, c, own, rest, wins):
    pairs = len(own)
    u, cols = own[0].shape[1:]
    n, seq, ins = wins.shape
    tile = TILE
    per = cols // tile
    at = lambda i, s, c: (jnp.where(i < per, c[0] * per + i, (1 - c[0]) * per + i - per), 0)
    return pl.pallas_call(
        functools.partial(pieces_kernel, pairs),
        grid_spec=pltpu.PrefetchScalarGridSpec(
            num_scalar_prefetch=2,
            grid=(2 * per,),
            in_specs=[pl.BlockSpec((2, u, tile), lambda i, s, c: (0, 0, jnp.minimum(i, per - 1)))] * pairs
            + [pl.BlockSpec((2, u, tile), lambda i, s, c: (0, 0, jnp.maximum(i - per, 0)))] * pairs
            + [pl.BlockSpec((n, seq, ins), lambda i, s, c: (0, 0, 0))],
            out_specs=pl.BlockSpec((tile, ins), at),
            scratch_shapes=[pltpu.VMEM((2 * pairs * u, tile), BF16)],
        ),
        out_shape=jax.ShapeDtypeStruct((2 * cols, ins), BF16),
        compiler_params=pltpu.CompilerParams(vmem_limit_bytes=60 * 2**20),
        cost_estimate=pl.CostEstimate(
            flops=4 * n * seq * cols * ins,
            bytes_accessed=2 * (4 * pairs * u * cols + n * seq * ins + 2 * cols * ins),
            transcendentals=0,
        ),
    )(starts, c.reshape(1), *own, *rest, wins)


def swap_dp(x, k, n_dp):
    return lax.ppermute(x, "dp", [(d, d ^ k) for d in range(n_dp)])


def project_in(kept, blocks, me):
    rows = blocks[0].shape[0]
    total = None
    for k, b in enumerate(blocks):
        a = lax.dynamic_slice_in_dim(kept, (me ^ k) * rows, rows, axis=1)
        t = jnp.dot(a, b, preferred_element_type=F32)
        total = t if total is None else total + t
    return total.astype(BF16)


def mask_acts(acts, lengths):
    keep = (jnp.arange(acts.shape[1], dtype=jnp.int32)[None, :] < lengths[:, None]).astype(acts.dtype)
    return (acts * keep[:, :, None])[0]


def general(n_dp, acts, out_grads, basis_in, basis_out, lengths):
    seq = acts.shape[1]
    me = lax.axis_index("dp")
    kept = mask_acts(acts, lengths)

    def exchange(x, width):
        parts = [lax.dynamic_slice_in_dim(x, (me ^ k) * width, width, axis=1) for k in range(n_dp)]
        return [parts[0]] + [swap_dp(parts[k], k, n_dp) for k in range(1, n_dp)]

    far = swap_dp(basis_in, 2, n_dp)
    blocks = [basis_in, swap_dp(basis_in, 1, n_dp), far, swap_dp(far, 1, n_dp)]
    in_local = project_in(kept, blocks, me)
    n_chunks = 3
    step = seq // n_chunks
    outs = []
    for j in range(n_chunks):
        g = out_grads[0, j * step : (j + 1) * step]
        whole = lax.all_gather(g, "tensor", axis=1, tiled=True)
        mine = jnp.concatenate(exchange(whole, whole.shape[1] // n_dp), axis=0)
        part = jnp.dot(mine, basis_out, preferred_element_type=F32)
        part = part.reshape(n_dp, step, -1)
        odd = swap_dp(part[1::2].astype(BF16), 1, n_dp)
        s0 = part[0] + odd[0].astype(F32)
        s2 = part[2] + odd[1].astype(F32)
        far = swap_dp(jnp.stack([s2, s0]).astype(BF16), 2, n_dp)
        even = jnp.stack([s0 + far[0].astype(F32), s2 + far[1].astype(F32)]).astype(BF16)
        rest = swap_dp(even, 1, n_dp)
        outs.append(jnp.stack([even[0], rest[0], even[1], rest[1]]))
    in_all = lax.all_gather(in_local, "tensor", axis=1, tiled=True)
    in_proj = jnp.stack(exchange(in_all, in_all.shape[1] // n_dp))
    out_proj = jnp.concatenate(outs, axis=1).reshape(n_dp * seq, -1)
    return squares(jnp.arange(n_dp, dtype=jnp.int32) * seq, out_proj, in_proj)


def home_pairs(hops, across=False):
    pairs = []
    for x in (0, 1):
        for c in (0, 1):
            d = 2 * x + c
            for w0, w1 in hops:
                z0, z1 = (w0, w1) if x == 0 else (3 - w0, 3 - w1)
                if across:
                    pairs.append((z0 * 4 + (d ^ 2), z1 * 4 + d))
                else:
                    pairs.append((z0 * 4 + d, z1 * 4 + d))
    return pairs


def send(x, hops, across=False):
    return lax.ppermute(x, ("tensor", "dp"), home_pairs(hops, across))


def to_home(x):
    return send(x, [(0, 0), (1, 1)], True)


def tie(v, *after):
    return lax.optimization_barrier((v,) + after)[0]


def swap(v, k=1):
    return swap_dp(v, k, 4)


def compact(cap, acts, grads, basis_in, basis_out, lens):
    seq = acts.shape[1]
    me = lax.axis_index("dp")
    z = lax.axis_index("tensor")
    x, c = me // 2, me % 2
    w = jnp.where(x == 0, z, 3 - z)
    m = STEPS
    u = cap // m
    c2 = min(m, -(-min(2 * seq, cap - 2 * MIN_LEN) // u))
    want_outer = c == x
    kept = mask_acts(acts, lax.dynamic_slice_in_dim(lens, me, 1))

    al = (lens + ALIGN - 1) // ALIGN * ALIGN
    off = jnp.stack([jnp.int32(0), al[0], cap - al[3] - al[2], cap - al[3]])

    pos = jnp.arange(c2 * u, dtype=jnp.int32)
    chunk = pos // u
    row = jnp.where(x == 0, chunk, m - 1 - chunk) * u + pos % u
    s = jnp.arange(seq, dtype=jnp.int32)

    def pick(n):
        return (row[:, None] == (off[n] + s)[None, :]) & (s < lens[n])[None, :]

    hot = jnp.concatenate([pick(me), pick(me ^ 1)], axis=1).astype(BF16)

    def pack(v):
        return jnp.dot(hot, v, preferred_element_type=F32).astype(BF16).reshape(c2, u, v.shape[1])

    def merged(own, others, i):
        t = None
        if i < c2:
            t = own[i]
        if m - 1 - i < c2:
            o = others[m - 1 - i]
            t = o if t is None else t + o
        return t

    def halves(outer, inner):
        mine = jnp.where(want_outer, outer, inner)
        return mine, swap(jnp.where(want_outer, inner, outer))

    packed = pack(grads)
    arrived = [None] * c2
    last = None
    for i in range(c2 - 1, -1, -1):
        arrived[i] = to_home(packed[i] if last is None else tie(packed[i], last))
        last = arrived[i]
    far_in = swap(tie(basis_in, last), 2)
    near_in = swap(tie(basis_in, arrived[c2 - 1]))
    far_near = swap(far_in)

    blocks, given, held, sums, fars = ([None] * m for _ in range(5))
    own, fa, fb, m1 = [None] * m, [None] * (m + 1), [None] * m, [None] * m

    def meet(i):
        outer = jnp.where(w == 0, own[i], jnp.where(w == 1, fa[i], jnp.where(w == 2, fb[i], fa[i + 1])))
        inner = jnp.where(w == 0, m1[i], jnp.where(w == 1, own[i], jnp.where(w == 2, fa[i], fb[i])))
        blocks[i] = halves(outer, inner)

    def product(i):
        given[i], held[i] = products(c, *blocks[i], basis_out)

    def add_core(i):
        sums[i] = held[i] + swap(given[i]).astype(F32)
        fars[i] = swap(sums[i].astype(BF16), 2)

    in_local = None
    for i in range(m):
        own[i] = merged(packed, arrived, i)
        v = own[i] if i == 0 else jnp.where(w == 2, fb[i - 1], own[i])
        fa[i] = send(tie(v, *([held[i - 3]] if i >= 3 else [])), [(0, 1), (1, 2)] + ([(2, 3)] if i else []))
        m1[i] = send(own[i], [(1, 0)])
        if i >= 1:
            meet(i - 1)
        if i >= 3:
            add_core(i - 3)
        after = []
        if i >= 2:
            after += blocks[i - 2]
            product(i - 2)
        if i >= 3:
            after.append(sums[i - 3])
        if i == m - 1:
            in_local = project_in(kept, [basis_in, near_in, far_in, far_near], me)
            after.append(in_local)
        fb[i] = send(tie(fa[i], *after), [(1, 2), (2, 3)])

    hc = in_local.shape[1] // 2
    in_mine = lax.dynamic_slice_in_dim(in_local, c * hc, hc, axis=1)
    in_given = lax.dynamic_slice_in_dim(in_local, (1 - c) * hc, hc, axis=1)
    in_packed = pack(jnp.concatenate([in_mine, swap(in_given)], axis=0))
    in_arrived = to_home(in_packed)
    in_own = jnp.concatenate([merged(in_packed, in_arrived, i) for i in range(m)], axis=0)

    after = [fb[m - 1], held[m - 3], blocks[m - 2][1]]
    fa[m] = send(tie(fb[m - 1], *after), [(2, 3)])
    r1 = send(tie(in_own, *after), [(0, 1), (1, 2)])
    i1 = send(in_own, [(1, 0)])
    add_core(m - 3)
    product(m - 2)
    meet(m - 1)
    r2 = send(tie(r1, fa[m], sums[m - 3], held[m - 2]), [(1, 2), (2, 3)])
    add_core(m - 2)
    product(m - 1)
    r3 = send(tie(r2, sums[m - 2], held[m - 1]), [(2, 3)])
    add_core(m - 1)
    outer = jnp.where(w == 0, in_own, jnp.where(w == 1, r1, jnp.where(w == 2, r2, r3)))
    inner = jnp.where(w == 0, i1, jnp.where(w == 1, in_own, jnp.where(w == 2, r1, r2)))
    mine, other = halves(outer, inner)
    in_t = jnp.where(c == 0, jnp.concatenate([mine, other], 1), jnp.concatenate([other, mine], 1))
    in_t = in_t.reshape(m, u, 2 * hc)
    in_t = jnp.where(x == 0, in_t, in_t[::-1]).reshape(cap, 2 * hc)

    mine, rest = [None] * (m // 2), [None] * (m // 2)
    for j in range(m // 2 - 1, -1, -1):
        k = m - 1 - j
        lo = jnp.where(x == 0, sums[j], sums[k]) + jnp.where(x == 0, fars[k], fars[j]).astype(F32)
        hi = jnp.where(x == 0, sums[k], sums[j]) + jnp.where(x == 0, fars[j], fars[k]).astype(F32)
        mine[j] = jnp.stack([lo, hi]).astype(BF16)
        rest[j] = swap(mine[j])

    ends = off + al
    starts = jnp.stack([off[0], off[1], ends[2] - seq, ends[3] - seq]).astype(jnp.int32)
    wins = []
    for n in range(4):
        rows = starts[n] + s
        valid = (rows >= off[n]) & (rows < off[n] + lens[n])
        win = lax.dynamic_slice_in_dim(in_t, starts[n], seq, axis=0)
        wins.append(jnp.where(valid[:, None], win, jnp.zeros_like(win)))
    return squares_of_pieces(starts, c, mine, rest, jnp.stack(wins))


def special(caps, acts, out_grads, basis_in, basis_out, lengths):
    me = lax.axis_index("dp")
    c = me % 2
    every = lax.all_gather(lengths, ("groups", "dp"), axis=0, tiled=True)
    g = out_grads[0]
    half = g.shape[1] // 2
    mine = lax.dynamic_slice_in_dim(g, c * half, half, axis=1)
    given = lax.dynamic_slice_in_dim(g, (1 - c) * half, half, axis=1)
    grads = jnp.concatenate([mine, swap_dp(given, 1, 4)], axis=0)
    totals = jnp.sum(((every + ALIGN - 1) // ALIGN * ALIGN).reshape(-1, 4), axis=1)
    need = jnp.max(totals)
    lens = lax.dynamic_slice_in_dim(every, lax.axis_index("groups") * 4, 4)
    out = jnp.zeros((basis_out.shape[1], basis_in.shape[0]), BF16)
    low = 0
    for cap in caps:
        todo = (need > low) & (need <= cap)
        low = cap

        def body(carry):
            now, a, g, b = lax.optimization_barrier((lens + 1 - carry[0], acts, grads, basis_in))
            return jnp.int32(0), compact(cap, a, g, b, basis_out, now)

        out = lax.while_loop(lambda carry: carry[0] == 1, body, (todo.astype(jnp.int32), out))[1]
    return out


def per_device(sizes, caps, acts, out_grads, basis_in, basis_out, lengths):
    if sizes == (4, 4):
        return special(caps, acts, out_grads, basis_in, basis_out, lengths)
    return general(sizes[1], acts, out_grads, basis_in, basis_out, lengths)


CAPS = (768, 832, 896, 960, 1152)


def solution(mesh):
    in_specs = (
        P(("groups", "dp"), None, None),
        P(("groups", "dp"), None, "tensor"),
        P(("groups", "dp"), "tensor"),
        P(("groups", "dp"), "tensor"),
        P(("groups", "dp")),
    )
    out_specs = P(("groups", "tensor"), "dp")
    sizes = (mesh.shape["tensor"], mesh.shape["dp"])
    return jax.shard_map(
        functools.partial(per_device, sizes, CAPS), mesh=mesh, in_specs=in_specs, out_specs=out_specs, check_vma=False
    )
```

```python
import functools

import jax
import jax.numpy as jnp
from jax import lax
from jax.experimental import pallas as pl
from jax.experimental.pallas import tpu as pltpu
from jax.sharding import PartitionSpec as P

F32 = jnp.float32
BF16 = jnp.bfloat16
ALIGN = 16
CHUNKS = (96, 80, 64, 48)
TILE = 256


def square_kernel(start_ref, out_ref, in_ref, c_ref):
    total = None
    for n in range(in_ref.shape[0]):
        rows = pl.ds(pl.multiple_of(start_ref[n], ALIGN), in_ref.shape[1])
        proj = lax.dot_general(out_ref[rows, :], in_ref[n], (((0,), (0,)), ((), ())), preferred_element_type=F32)
        total = proj * proj if total is None else total + proj * proj
    c_ref[...] = total.astype(c_ref.dtype)


def squares(starts, out_proj, in_proj):
    tokens, cols = out_proj.shape
    n, seq, ins = in_proj.shape
    tile = cols
    for t in (512, 256, 128):
        if cols % t == 0:
            tile = t
            break
    return pl.pallas_call(
        square_kernel,
        grid_spec=pltpu.PrefetchScalarGridSpec(
            num_scalar_prefetch=1,
            grid=(cols // tile,),
            in_specs=[
                pl.BlockSpec((tokens, tile), lambda i, s: (0, i)),
                pl.BlockSpec((n, seq, ins), lambda i, s: (0, 0, 0)),
            ],
            out_specs=pl.BlockSpec((tile, ins), lambda i, s: (i, 0)),
        ),
        out_shape=jax.ShapeDtypeStruct((cols, ins), BF16),
        compiler_params=pltpu.CompilerParams(vmem_limit_bytes=60 * 2**20),
        cost_estimate=pl.CostEstimate(
            flops=2 * n * seq * cols * ins, bytes_accessed=2 * (n * seq * (cols + ins) + cols * ins), transcendentals=0
        ),
    )(starts, out_proj, in_proj)


def product_kernel(*refs):
    x_refs, basis_ref, given_ref, held_ref, rows_ref = refs[:4], refs[4], refs[5], refs[6], refs[7]
    r = x_refs[0].shape[0]

    @pl.when(pl.program_id(0) == 0)
    def _():
        for at, k in enumerate((1, 3, 0, 2)):
            rows_ref[at * r : (at + 1) * r, :] = x_refs[k][...]

    total = jnp.dot(rows_ref[...], basis_ref[...], preferred_element_type=F32)
    given_ref[...] = total[: 2 * r].astype(given_ref.dtype)
    held_ref[...] = total[2 * r :]


def products(blocks, basis):
    r, depth = blocks[0].shape
    cols = basis.shape[1]
    return pl.pallas_call(
        product_kernel,
        grid=(cols // TILE,),
        in_specs=[pl.BlockSpec((r, depth), lambda i: (0, 0))] * 4 + [pl.BlockSpec((depth, TILE), lambda i: (0, i))],
        out_specs=[pl.BlockSpec((2 * r, TILE), lambda i: (0, i))] * 2,
        out_shape=[jax.ShapeDtypeStruct((2 * r, cols), BF16), jax.ShapeDtypeStruct((2 * r, cols), F32)],
        scratch_shapes=[pltpu.VMEM((4 * r, depth), BF16)],
        compiler_params=pltpu.CompilerParams(vmem_limit_bytes=32 * 2**20),
        cost_estimate=pl.CostEstimate(flops=1, bytes_accessed=1, transcendentals=0),
    )(*blocks, basis)


def pieces_kernel(n_chunks, *refs):
    own, rest, in_ref, out_ref, rows_ref = refs[:n_chunks], refs[n_chunks : 2 * n_chunks], refs[-3], refs[-2], refs[-1]
    total = None
    for k in range(4):
        at = 0
        for part in own if k % 2 == 0 else rest:
            r = part.shape[0] // 2
            rows_ref[k, at : at + r, :] = part[(k // 2) * r : (k // 2 + 1) * r, :]
            at += r
        proj = lax.dot_general(rows_ref[k], in_ref[k], (((0,), (0,)), ((), ())), preferred_element_type=F32)
        total = proj * proj if total is None else total + proj * proj
    out_ref[...] = total.astype(out_ref.dtype)


def squares_of_pieces(own, rest, in_proj):
    cols = own[0].shape[1]
    n, seq, ins = in_proj.shape
    return pl.pallas_call(
        functools.partial(pieces_kernel, len(own)),
        grid=(cols // TILE,),
        in_specs=[pl.BlockSpec((p.shape[0], TILE), lambda i: (0, i)) for p in own + rest]
        + [pl.BlockSpec((n, seq, ins), lambda i: (0, 0, 0))],
        out_specs=pl.BlockSpec((TILE, ins), lambda i: (i, 0)),
        out_shape=jax.ShapeDtypeStruct((cols, ins), BF16),
        scratch_shapes=[pltpu.VMEM((n, seq, TILE), BF16)],
        compiler_params=pltpu.CompilerParams(vmem_limit_bytes=60 * 2**20),
        cost_estimate=pl.CostEstimate(flops=1, bytes_accessed=1, transcendentals=0),
    )(*own, *rest, in_proj)


def swap_dp(x, k, n_dp):
    return lax.ppermute(x, "dp", [(d, d ^ k) for d in range(n_dp)])


def project_in(kept, blocks, me):
    rows = blocks[0].shape[0]
    total = None
    for k, b in enumerate(blocks):
        a = lax.dynamic_slice_in_dim(kept, (me ^ k) * rows, rows, axis=1)
        t = jnp.dot(a, b, preferred_element_type=F32)
        total = t if total is None else total + t
    return total.astype(BF16)


def mask_acts(acts, lengths):
    keep = (jnp.arange(acts.shape[1], dtype=jnp.int32)[None, :] < lengths[:, None]).astype(acts.dtype)
    return (acts * keep[:, :, None])[0]


def general(n_dp, acts, out_grads, basis_in, basis_out, lengths):
    seq = acts.shape[1]
    me = lax.axis_index("dp")
    kept = mask_acts(acts, lengths)

    def exchange(x, width):
        parts = [lax.dynamic_slice_in_dim(x, (me ^ k) * width, width, axis=1) for k in range(n_dp)]
        return [parts[0]] + [swap_dp(parts[k], k, n_dp) for k in range(1, n_dp)]

    far = swap_dp(basis_in, 2, n_dp)
    blocks = [basis_in, swap_dp(basis_in, 1, n_dp), far, swap_dp(far, 1, n_dp)]
    in_local = project_in(kept, blocks, me)
    n_chunks = 3
    step = seq // n_chunks
    outs = []
    for j in range(n_chunks):
        g = out_grads[0, j * step : (j + 1) * step]
        whole = lax.all_gather(g, "tensor", axis=1, tiled=True)
        mine = jnp.concatenate(exchange(whole, whole.shape[1] // n_dp), axis=0)
        part = jnp.dot(mine, basis_out, preferred_element_type=F32)
        part = part.reshape(n_dp, step, -1)
        odd = swap_dp(part[1::2].astype(BF16), 1, n_dp)
        s0 = part[0] + odd[0].astype(F32)
        s2 = part[2] + odd[1].astype(F32)
        far = swap_dp(jnp.stack([s2, s0]).astype(BF16), 2, n_dp)
        even = jnp.stack([s0 + far[0].astype(F32), s2 + far[1].astype(F32)]).astype(BF16)
        rest = swap_dp(even, 1, n_dp)
        outs.append(jnp.stack([even[0], rest[0], even[1], rest[1]]))
    in_all = lax.all_gather(in_local, "tensor", axis=1, tiled=True)
    in_proj = jnp.stack(exchange(in_all, in_all.shape[1] // n_dp))
    out_proj = jnp.concatenate(outs, axis=1).reshape(n_dp * seq, -1)
    return squares(jnp.arange(n_dp, dtype=jnp.int32) * seq, out_proj, in_proj)


def tie(v, *after):
    return lax.optimization_barrier((v,) + after)[0]


def special(acts, out_grads, basis_in, basis_out, lengths):
    me = lax.axis_index("dp")
    z = lax.axis_index("tensor")
    swap = lambda v, k: swap_dp(v, k, 4)
    shift = lambda v, k: lax.ppermute(v, "tensor", [(i, (i + k) % 4) for i in range(4)])

    far = swap(basis_in, 2)
    blocks = [basis_in, swap(basis_in, 1), far, swap(far, 1)]
    in_local = project_in(mask_acts(acts, lengths), blocks, me)

    wholes = []
    at = 0
    for r in CHUNKS:
        wholes.append(lax.all_gather(out_grads[0, at : at + r], "tensor", axis=0))
        at += r

    def parts_of(whole):
        return [lax.dynamic_index_in_dim(whole, me ^ k, 0, keepdims=False) for k in range(4)]

    def spread(parts):
        return [parts[0]] + [swap(parts[k], k) for k in range(1, 4)]

    n = len(CHUNKS)
    own, rest = [], []
    parts = [None] * n
    parts[0] = parts_of(tie(wholes[0], far))
    mine = spread(parts[0])
    after = [in_local]
    for i, r in enumerate(CHUNKS):
        if i >= 1 and i + 1 < n:
            parts[i + 1] = parts_of(wholes[i + 1])
            after += parts[i + 1]
        mine[0] = tie(mine[0], *after)
        given, held = products(mine, basis_out)
        sums = held + swap(given, 1).astype(F32)
        far = swap(sums.astype(BF16), 2)
        after = [far]
        if i == 0:
            parts[1] = parts_of(tie(wholes[1], in_local))
            got = [in_local] + [shift(in_local, k) for k in (1, 2, 3)]
            after += got
        if i == 1:
            in_parts = []
            for k in range(4):
                by = (z - (me ^ k)) % 4
                in_parts.append(lax.select_n(by, *got))
            in_all = [in_parts[0]] + [swap(in_parts[k], k) for k in range(1, 4)]
            after += in_all
        if i + 1 < n:
            mine = spread(parts[i + 1])
        full = jnp.concatenate([sums[:r] + far[r:].astype(F32), sums[r:] + far[:r].astype(F32)]).astype(BF16)
        own.append(full)
        rest.append(swap(full, 1))
    in_all = jnp.stack(in_all)
    return squares_of_pieces(own, rest, in_all)


def per_device(sizes, acts, out_grads, basis_in, basis_out, lengths):
    if sizes == (4, 4) and sum(CHUNKS) == acts.shape[1]:
        return special(acts, out_grads, basis_in, basis_out, lengths)
    return general(sizes[1], acts, out_grads, basis_in, basis_out, lengths)


def solution(mesh):
    in_specs = (
        P(("groups", "dp"), None, None),
        P(("groups", "dp"), None, "tensor"),
        P(("groups", "dp"), "tensor"),
        P(("groups", "dp"), "tensor"),
        P(("groups", "dp")),
    )
    out_specs = P(("groups", "tensor"), "dp")
    sizes = (mesh.shape["tensor"], mesh.shape["dp"])
    return jax.shard_map(
        functools.partial(per_device, sizes), mesh=mesh, in_specs=in_specs, out_specs=out_specs, check_vma=False
    )
```

```python
import functools

import jax
import jax.numpy as jnp
from jax import lax
from jax.experimental import pallas as pl
from jax.experimental.pallas import tpu as pltpu
from jax.sharding import PartitionSpec as P

F32 = jnp.float32
BF16 = jnp.bfloat16
MIN_LEN = 96
ALIGN = 16
TILE = 256
STEPS = 4


def square_kernel(start_ref, out_ref, in_ref, c_ref):
    total = None
    for n in range(in_ref.shape[0]):
        rows = pl.ds(pl.multiple_of(start_ref[n], ALIGN), in_ref.shape[1])
        proj = lax.dot_general(out_ref[rows, :], in_ref[n], (((0,), (0,)), ((), ())), preferred_element_type=F32)
        total = proj * proj if total is None else total + proj * proj
    c_ref[...] = total.astype(c_ref.dtype)


def squares(starts, out_proj, in_proj):
    tokens, cols = out_proj.shape
    n, seq, ins = in_proj.shape
    tile = cols
    for t in (512, 256, 128):
        if cols % t == 0:
            tile = t
            break
    return pl.pallas_call(
        square_kernel,
        grid_spec=pltpu.PrefetchScalarGridSpec(
            num_scalar_prefetch=1,
            grid=(cols // tile,),
            in_specs=[
                pl.BlockSpec((tokens, tile), lambda i, s: (0, i)),
                pl.BlockSpec((n, seq, ins), lambda i, s: (0, 0, 0)),
            ],
            out_specs=pl.BlockSpec((tile, ins), lambda i, s: (i, 0)),
        ),
        out_shape=jax.ShapeDtypeStruct((cols, ins), BF16),
        compiler_params=pltpu.CompilerParams(vmem_limit_bytes=60 * 2**20),
        cost_estimate=pl.CostEstimate(
            flops=2 * n * seq * cols * ins, bytes_accessed=2 * (n * seq * (cols + ins) + cols * ins), transcendentals=0
        ),
    )(starts, out_proj, in_proj)


def product_kernel(c_ref, mine_ref, other_ref, b_mine_ref, b_other_ref, given_ref, held_ref):
    i = pl.program_id(0)
    total = jnp.dot(mine_ref[...], b_mine_ref[...], preferred_element_type=F32)
    total = total + jnp.dot(other_ref[...], b_other_ref[...], preferred_element_type=F32)

    @pl.when(i < pl.num_programs(0) // 2)
    def _():
        given_ref[...] = total.astype(given_ref.dtype)

    @pl.when(i >= pl.num_programs(0) // 2)
    def _():
        held_ref[...] = total


def products(c, mine, other, basis):
    rows, depth = mine.shape
    cols = basis.shape[1] // 2
    tile = 896 if cols % 896 == 0 else TILE
    per = cols // tile
    at = lambda i, c: jnp.where(i < per, (1 - c[0]) * per + i, c[0] * per + i - per)
    return pl.pallas_call(
        product_kernel,
        grid_spec=pltpu.PrefetchScalarGridSpec(
            num_scalar_prefetch=1,
            grid=(2 * per,),
            in_specs=[
                pl.BlockSpec((rows, depth), lambda i, c: (0, 0)),
                pl.BlockSpec((rows, depth), lambda i, c: (0, 0)),
                pl.BlockSpec((depth, tile), lambda i, c: (c[0], at(i, c))),
                pl.BlockSpec((depth, tile), lambda i, c: (1 - c[0], at(i, c))),
            ],
            out_specs=[
                pl.BlockSpec((rows, tile), lambda i, c: (0, jnp.minimum(i, per - 1))),
                pl.BlockSpec((rows, tile), lambda i, c: (0, jnp.maximum(i - per, 0))),
            ],
        ),
        out_shape=[jax.ShapeDtypeStruct((rows, cols), BF16), jax.ShapeDtypeStruct((rows, cols), F32)],
        compiler_params=pltpu.CompilerParams(vmem_limit_bytes=36 * 2**20),
        cost_estimate=pl.CostEstimate(flops=1, bytes_accessed=1, transcendentals=0),
    )(c.reshape(1), mine, other, basis, basis)


def pieces_kernel(pairs, start_ref, c_ref, *refs):
    own, rest, in_ref, out_ref, held = refs[:pairs], refs[pairs : 2 * pairs], refs[-3], refs[-2], refs[-1]
    i = pl.program_id(0)
    u = own[0].shape[1]

    def fill(parts):
        for j, part in enumerate(parts):
            held[j * u : (j + 1) * u, :] = part[0]
            k = 2 * pairs - 1 - j
            held[k * u : (k + 1) * u, :] = part[1]

    @pl.when(i < pl.num_programs(0) // 2)
    def _():
        fill(own)

    @pl.when(i >= pl.num_programs(0) // 2)
    def _():
        fill(rest)

    total = None
    for n in range(in_ref.shape[0]):
        rows = pl.ds(pl.multiple_of(start_ref[n], ALIGN), in_ref.shape[1])
        proj = lax.dot_general(held[rows, :], in_ref[n], (((0,), (0,)), ((), ())), preferred_element_type=F32)
        total = proj * proj if total is None else total + proj * proj
    out_ref[...] = total.astype(out_ref.dtype)


def squares_of_pieces(starts, c, own, rest, wins):
    pairs = len(own)
    u, cols = own[0].shape[1:]
    n, seq, ins = wins.shape
    tile = TILE
    per = cols // tile
    at = lambda i, s, c: (jnp.where(i < per, c[0] * per + i, (1 - c[0]) * per + i - per), 0)
    return pl.pallas_call(
        functools.partial(pieces_kernel, pairs),
        grid_spec=pltpu.PrefetchScalarGridSpec(
            num_scalar_prefetch=2,
            grid=(2 * per,),
            in_specs=[pl.BlockSpec((2, u, tile), lambda i, s, c: (0, 0, jnp.minimum(i, per - 1)))] * pairs
            + [pl.BlockSpec((2, u, tile), lambda i, s, c: (0, 0, jnp.maximum(i - per, 0)))] * pairs
            + [pl.BlockSpec((n, seq, ins), lambda i, s, c: (0, 0, 0))],
            out_specs=pl.BlockSpec((tile, ins), at),
            scratch_shapes=[pltpu.VMEM((2 * pairs * u, tile), BF16)],
        ),
        out_shape=jax.ShapeDtypeStruct((2 * cols, ins), BF16),
        compiler_params=pltpu.CompilerParams(vmem_limit_bytes=40 * 2**20),
        cost_estimate=pl.CostEstimate(flops=1, bytes_accessed=1, transcendentals=0),
    )(starts, c.reshape(1), *own, *rest, wins)


def swap_dp(x, k, n_dp):
    return lax.ppermute(x, "dp", [(d, d ^ k) for d in range(n_dp)])


def project_in(kept, blocks, me):
    rows = blocks[0].shape[0]
    total = None
    for k, b in enumerate(blocks):
        a = lax.dynamic_slice_in_dim(kept, (me ^ k) * rows, rows, axis=1)
        t = jnp.dot(a, b, preferred_element_type=F32)
        total = t if total is None else total + t
    return total.astype(BF16)


def mask_acts(acts, lengths):
    keep = (jnp.arange(acts.shape[1], dtype=jnp.int32)[None, :] < lengths[:, None]).astype(acts.dtype)
    return (acts * keep[:, :, None])[0]


def general(n_dp, acts, out_grads, basis_in, basis_out, lengths):
    seq = acts.shape[1]
    me = lax.axis_index("dp")
    kept = mask_acts(acts, lengths)

    def exchange(x, width):
        parts = [lax.dynamic_slice_in_dim(x, (me ^ k) * width, width, axis=1) for k in range(n_dp)]
        return [parts[0]] + [swap_dp(parts[k], k, n_dp) for k in range(1, n_dp)]

    far = swap_dp(basis_in, 2, n_dp)
    blocks = [basis_in, swap_dp(basis_in, 1, n_dp), far, swap_dp(far, 1, n_dp)]
    in_local = project_in(kept, blocks, me)
    n_chunks = 3
    step = seq // n_chunks
    outs = []
    for j in range(n_chunks):
        g = out_grads[0, j * step : (j + 1) * step]
        whole = lax.all_gather(g, "tensor", axis=1, tiled=True)
        mine = jnp.concatenate(exchange(whole, whole.shape[1] // n_dp), axis=0)
        part = jnp.dot(mine, basis_out, preferred_element_type=F32)
        part = part.reshape(n_dp, step, -1)
        odd = swap_dp(part[1::2].astype(BF16), 1, n_dp)
        s0 = part[0] + odd[0].astype(F32)
        s2 = part[2] + odd[1].astype(F32)
        far = swap_dp(jnp.stack([s2, s0]).astype(BF16), 2, n_dp)
        even = jnp.stack([s0 + far[0].astype(F32), s2 + far[1].astype(F32)]).astype(BF16)
        rest = swap_dp(even, 1, n_dp)
        outs.append(jnp.stack([even[0], rest[0], even[1], rest[1]]))
    in_all = lax.all_gather(in_local, "tensor", axis=1, tiled=True)
    in_proj = jnp.stack(exchange(in_all, in_all.shape[1] // n_dp))
    out_proj = jnp.concatenate(outs, axis=1).reshape(n_dp * seq, -1)
    return squares(jnp.arange(n_dp, dtype=jnp.int32) * seq, out_proj, in_proj)


def home_pairs(hops, across=False):
    pairs = []
    for x in (0, 1):
        for c in (0, 1):
            d = 2 * x + c
            for w0, w1 in hops:
                z0, z1 = (w0, w1) if x == 0 else (3 - w0, 3 - w1)
                if across:
                    pairs.append((z0 * 4 + (d ^ 2), z1 * 4 + d))
                else:
                    pairs.append((z0 * 4 + d, z1 * 4 + d))
    return pairs


def send(x, hops, across=False):
    return lax.ppermute(x, ("tensor", "dp"), home_pairs(hops, across))


def to_home(x):
    return send(x, [(0, 0), (1, 1)], True)


def tie(v, *after):
    return lax.optimization_barrier((v,) + after)[0]


def swap(v, k=1):
    return swap_dp(v, k, 4)


def compact(cap, acts, grads, basis_in, basis_out, lens):
    seq = acts.shape[1]
    me = lax.axis_index("dp")
    z = lax.axis_index("tensor")
    x, c = me // 2, me % 2
    w = jnp.where(x == 0, z, 3 - z)
    m = STEPS
    u = cap // m
    c2 = min(m, -(-min(2 * seq, cap - 2 * MIN_LEN) // u))
    want_outer = c == x
    kept = mask_acts(acts, lax.dynamic_slice_in_dim(lens, me, 1))

    al = (lens + ALIGN - 1) // ALIGN * ALIGN
    off = jnp.stack([jnp.int32(0), al[0], cap - al[3] - al[2], cap - al[3]])

    pos = jnp.arange(c2 * u, dtype=jnp.int32)
    chunk = pos // u
    row = jnp.where(x == 0, chunk, m - 1 - chunk) * u + pos % u
    s = jnp.arange(seq, dtype=jnp.int32)

    def pick(n):
        return (row[:, None] == (off[n] + s)[None, :]) & (s < lens[n])[None, :]

    hot = jnp.concatenate([pick(me), pick(me ^ 1)], axis=1).astype(BF16)

    def pack(v):
        return jnp.dot(hot, v, preferred_element_type=F32).astype(BF16).reshape(c2, u, v.shape[1])

    def merged(own, others, i):
        t = None
        if i < c2:
            t = own[i]
        if m - 1 - i < c2:
            o = others[m - 1 - i]
            t = o if t is None else t + o
        return t

    def halves(outer, inner):
        mine = jnp.where(want_outer, outer, inner)
        return mine, swap(jnp.where(want_outer, inner, outer))

    packed = pack(grads)
    arrived = [None] * c2
    last = None
    for i in range(c2 - 1, -1, -1):
        arrived[i] = to_home(packed[i] if last is None else tie(packed[i], last))
        last = arrived[i]
    far_in = swap(tie(basis_in, last), 2)
    near_in = swap(tie(basis_in, arrived[c2 - 1]))
    far_near = swap(far_in)

    blocks, given, held, sums, fars = ([None] * m for _ in range(5))
    own, fa, fb, m1 = [None] * m, [None] * (m + 1), [None] * m, [None] * m

    def meet(i):
        outer = jnp.where(w == 0, own[i], jnp.where(w == 1, fa[i], jnp.where(w == 2, fb[i], fa[i + 1])))
        inner = jnp.where(w == 0, m1[i], jnp.where(w == 1, own[i], jnp.where(w == 2, fa[i], fb[i])))
        blocks[i] = halves(outer, inner)

    def product(i):
        given[i], held[i] = products(c, *blocks[i], basis_out)

    def add_core(i):
        sums[i] = held[i] + swap(given[i]).astype(F32)
        fars[i] = swap(sums[i].astype(BF16), 2)

    in_local = None
    for i in range(m):
        own[i] = merged(packed, arrived, i)
        v = own[i] if i == 0 else jnp.where(w == 2, fb[i - 1], own[i])
        fa[i] = send(tie(v, *([held[i - 3]] if i >= 3 else [])), [(0, 1), (1, 2)] + ([(2, 3)] if i else []))
        m1[i] = send(own[i], [(1, 0)])
        if i >= 1:
            meet(i - 1)
        if i >= 3:
            add_core(i - 3)
        after = []
        if i >= 2:
            after += blocks[i - 2]
            product(i - 2)
        if i >= 3:
            after.append(sums[i - 3])
        if i == m - 1:
            in_local = project_in(kept, [basis_in, near_in, far_in, far_near], me)
            after.append(in_local)
        fb[i] = send(tie(fa[i], *after), [(1, 2), (2, 3)])

    hc = in_local.shape[1] // 2
    in_mine = lax.dynamic_slice_in_dim(in_local, c * hc, hc, axis=1)
    in_given = lax.dynamic_slice_in_dim(in_local, (1 - c) * hc, hc, axis=1)
    in_packed = pack(jnp.concatenate([in_mine, swap(in_given)], axis=0))
    in_arrived = to_home(in_packed)
    in_own = jnp.concatenate([merged(in_packed, in_arrived, i) for i in range(m)], axis=0)

    after = [fb[m - 1], held[m - 3], fars[m - 4], blocks[m - 2][1]]
    fa[m] = send(tie(fb[m - 1], *after), [(2, 3)])
    r1 = send(tie(in_own, *after), [(0, 1), (1, 2)])
    i1 = send(in_own, [(1, 0)])
    add_core(m - 3)
    blocks[m - 2] = (tie(blocks[m - 2][0], fb[m - 1]), blocks[m - 2][1])
    product(m - 2)
    meet(m - 1)
    r2 = send(tie(r1, fa[m], fars[m - 3], held[m - 2]), [(1, 2), (2, 3)])
    add_core(m - 2)
    product(m - 1)
    r3 = send(tie(r2, sums[m - 2], held[m - 1]), [(2, 3)])
    add_core(m - 1)
    outer = jnp.where(w == 0, in_own, jnp.where(w == 1, r1, jnp.where(w == 2, r2, r3)))
    inner = jnp.where(w == 0, i1, jnp.where(w == 1, in_own, jnp.where(w == 2, r1, r2)))
    mine, other = halves(outer, inner)
    in_t = jnp.where(c == 0, jnp.concatenate([mine, other], 1), jnp.concatenate([other, mine], 1))
    in_t = in_t.reshape(m, u, 2 * hc)
    in_t = jnp.where(x == 0, in_t, in_t[::-1]).reshape(cap, 2 * hc)

    mine, rest = [None] * (m // 2), [None] * (m // 2)
    for j in range(m // 2 - 1, -1, -1):
        k = m - 1 - j
        lo = jnp.where(x == 0, sums[j], sums[k]) + jnp.where(x == 0, fars[k], fars[j]).astype(F32)
        hi = jnp.where(x == 0, sums[k], sums[j]) + jnp.where(x == 0, fars[j], fars[k]).astype(F32)
        mine[j] = jnp.stack([lo, hi]).astype(BF16)
        rest[j] = swap(mine[j])

    ends = off + al
    starts = jnp.stack([off[0], off[1], ends[2] - seq, ends[3] - seq]).astype(jnp.int32)
    wins = []
    for n in range(4):
        rows = starts[n] + s
        valid = (rows >= off[n]) & (rows < off[n] + lens[n])
        win = lax.dynamic_slice_in_dim(in_t, starts[n], seq, axis=0)
        wins.append(jnp.where(valid[:, None], win, jnp.zeros_like(win)))
    return squares_of_pieces(starts, c, mine, rest, jnp.stack(wins))


def special(caps, acts, out_grads, basis_in, basis_out, lengths):
    me = lax.axis_index("dp")
    c = me % 2
    every = lax.all_gather(lengths, ("groups", "dp"), axis=0, tiled=True)
    g = out_grads[0]
    half = g.shape[1] // 2
    mine = lax.dynamic_slice_in_dim(g, c * half, half, axis=1)
    given = lax.dynamic_slice_in_dim(g, (1 - c) * half, half, axis=1)
    grads = jnp.concatenate([mine, swap_dp(given, 1, 4)], axis=0)
    totals = jnp.sum(((every + ALIGN - 1) // ALIGN * ALIGN).reshape(-1, 4), axis=1)
    need = jnp.max(totals)
    lens = lax.dynamic_slice_in_dim(every, lax.axis_index("groups") * 4, 4)
    index = jnp.int32(0)
    for cap in caps[:-1]:
        index = index + (need > cap).astype(jnp.int32)
    branches = [functools.partial(compact, cap) for cap in caps]
    return lax.switch(index, branches, acts, grads, basis_in, basis_out, lens)


def per_device(sizes, caps, acts, out_grads, basis_in, basis_out, lengths):
    if sizes == (4, 4):
        return special(caps, acts, out_grads, basis_in, basis_out, lengths)
    return general(sizes[1], acts, out_grads, basis_in, basis_out, lengths)


CAPS = (768, 832, 896, 960, 1152)


def solution(mesh):
    in_specs = (
        P(("groups", "dp"), None, None),
        P(("groups", "dp"), None, "tensor"),
        P(("groups", "dp"), "tensor"),
        P(("groups", "dp"), "tensor"),
        P(("groups", "dp")),
    )
    out_specs = P(("groups", "tensor"), "dp")
    sizes = (mesh.shape["tensor"], mesh.shape["dp"])
    return jax.shard_map(
        functools.partial(per_device, sizes, CAPS), mesh=mesh, in_specs=in_specs, out_specs=out_specs, check_vma=False
    )
```

```python
import functools

import jax
import jax.numpy as jnp
from jax import lax
from jax.experimental import pallas as pl
from jax.experimental.pallas import tpu as pltpu
from jax.sharding import PartitionSpec as P

F32 = jnp.float32
BF16 = jnp.bfloat16
MIN_LEN = 96
ALIGN = 16
TILE = 256
STEPS = 4


def square_kernel(start_ref, out_ref, in_ref, c_ref):
    total = None
    for n in range(in_ref.shape[0]):
        rows = pl.ds(pl.multiple_of(start_ref[n], ALIGN), in_ref.shape[1])
        proj = lax.dot_general(out_ref[rows, :], in_ref[n], (((0,), (0,)), ((), ())), preferred_element_type=F32)
        total = proj * proj if total is None else total + proj * proj
    c_ref[...] = total.astype(c_ref.dtype)


def squares(starts, out_proj, in_proj):
    tokens, cols = out_proj.shape
    n, seq, ins = in_proj.shape
    tile = cols
    for t in (512, 256, 128):
        if cols % t == 0:
            tile = t
            break
    return pl.pallas_call(
        square_kernel,
        grid_spec=pltpu.PrefetchScalarGridSpec(
            num_scalar_prefetch=1,
            grid=(cols // tile,),
            in_specs=[
                pl.BlockSpec((tokens, tile), lambda i, s: (0, i)),
                pl.BlockSpec((n, seq, ins), lambda i, s: (0, 0, 0)),
            ],
            out_specs=pl.BlockSpec((tile, ins), lambda i, s: (i, 0)),
        ),
        out_shape=jax.ShapeDtypeStruct((cols, ins), BF16),
        compiler_params=pltpu.CompilerParams(vmem_limit_bytes=60 * 2**20),
        cost_estimate=pl.CostEstimate(
            flops=2 * n * seq * cols * ins, bytes_accessed=2 * (n * seq * (cols + ins) + cols * ins), transcendentals=0
        ),
    )(starts, out_proj, in_proj)


def product_kernel(c_ref, mine_ref, other_ref, b_mine_ref, b_other_ref, given_ref, held_ref):
    i = pl.program_id(0)
    total = jnp.dot(mine_ref[...], b_mine_ref[...], preferred_element_type=F32)
    total = total + jnp.dot(other_ref[...], b_other_ref[...], preferred_element_type=F32)

    @pl.when(i < pl.num_programs(0) // 2)
    def _():
        given_ref[...] = total.astype(given_ref.dtype)

    @pl.when(i >= pl.num_programs(0) // 2)
    def _():
        held_ref[...] = total


def products(c, mine, other, basis):
    rows, depth = mine.shape
    cols = basis.shape[1] // 2
    tile = 896 if cols % 896 == 0 else TILE
    per = cols // tile
    at = lambda i, c: jnp.where(i < per, (1 - c[0]) * per + i, c[0] * per + i - per)
    return pl.pallas_call(
        product_kernel,
        grid_spec=pltpu.PrefetchScalarGridSpec(
            num_scalar_prefetch=1,
            grid=(2 * per,),
            in_specs=[
                pl.BlockSpec((rows, depth), lambda i, c: (0, 0)),
                pl.BlockSpec((rows, depth), lambda i, c: (0, 0)),
                pl.BlockSpec((depth, tile), lambda i, c: (c[0], at(i, c))),
                pl.BlockSpec((depth, tile), lambda i, c: (1 - c[0], at(i, c))),
            ],
            out_specs=[
                pl.BlockSpec((rows, tile), lambda i, c: (0, jnp.minimum(i, per - 1))),
                pl.BlockSpec((rows, tile), lambda i, c: (0, jnp.maximum(i - per, 0))),
            ],
        ),
        out_shape=[jax.ShapeDtypeStruct((rows, cols), BF16), jax.ShapeDtypeStruct((rows, cols), F32)],
        compiler_params=pltpu.CompilerParams(vmem_limit_bytes=36 * 2**20),
        cost_estimate=pl.CostEstimate(flops=1, bytes_accessed=1, transcendentals=0),
    )(c.reshape(1), mine, other, basis, basis)


def places(cap, lens):
    al = [(v + ALIGN - 1) // ALIGN * ALIGN for v in lens]
    return [jnp.int32(0), al[0], cap - al[3] - al[2], cap - al[3]], al


def choose(me, values):
    out = values[0]
    for k in range(1, len(values)):
        out = jnp.where(me == k, values[k], out)
    return out


def pack_kernel(cap, lens_ref, me_ref, own_ref, next_ref, *outs):
    me = me_ref[0]
    lens = [lens_ref[k] for k in range(4)]
    off = places(cap, lens)[0]
    seq = own_ref.shape[0]
    u = cap // STEPS
    for i in range(len(outs) if len(outs) > 1 else outs[0].shape[0]):
        first = jnp.where(me < 2, i, STEPS - 1 - i) * u
        row = first + lax.broadcasted_iota(jnp.int32, (u, seq), 0)
        s = lax.broadcasted_iota(jnp.int32, (u, seq), 1)
        total = None
        for n, ref in ((me, own_ref), (me ^ 1, next_ref)):
            hit = (row == s + choose(n, off)) & (s < choose(n, lens))
            t = jnp.dot(jnp.where(hit, 1.0, 0.0).astype(BF16), ref[...], preferred_element_type=F32)
            total = t if total is None else total + t
        if len(outs) > 1:
            outs[i][...] = total.astype(BF16)
        else:
            outs[0][i] = total.astype(BF16)


def packs(cap, count, split, lens, me, own, following):
    u, width = cap // STEPS, own.shape[1]
    if split and count > 1:
        shapes = [jax.ShapeDtypeStruct((u, width), BF16)] * count
    else:
        shapes = [jax.ShapeDtypeStruct((count, u, width), BF16)]
    out = pl.pallas_call(
        functools.partial(pack_kernel, cap),
        in_specs=[pl.BlockSpec(memory_space=pltpu.SMEM)] * 2 + [pl.BlockSpec(memory_space=pltpu.VMEM)] * 2,
        out_specs=[pl.BlockSpec(memory_space=pltpu.VMEM)] * len(shapes),
        out_shape=shapes,
        compiler_params=pltpu.CompilerParams(vmem_limit_bytes=24 * 2**20),
        cost_estimate=pl.CostEstimate(flops=1, bytes_accessed=1, transcendentals=0),
    )(lens, me.reshape(1), own, following)
    return out if split else out[0]


def pieces_kernel(cap, pairs, lens_ref, me_ref, *refs):
    parts, mine_ref, other_ref = refs[:pairs], refs[pairs], refs[pairs + 1]
    out_ref, held, rows_in, wins, total = refs[-5:]
    u = cap // STEPS
    me = me_ref[0]
    lens = [lens_ref[k] for k in range(4)]
    off, al = places(cap, lens)
    seq = wins.shape[1]
    starts = [off[0], off[1], off[2] + al[2] - seq, off[3] + al[3] - seq]

    @pl.when(pl.program_id(0) == 0)
    def _():
        c, hc = me % 2, mine_ref.shape[1]
        for p in range(STEPS):
            at = pl.ds(pl.multiple_of(jnp.where(me < 2, p, STEPS - 1 - p) * u, ALIGN), u)
            rows_in[at, pl.ds(pl.multiple_of(c * hc, 128), hc)] = mine_ref[p * u : (p + 1) * u, :]
            rows_in[at, pl.ds(pl.multiple_of((1 - c) * hc, 128), hc)] = other_ref[p * u : (p + 1) * u, :]
        for n in range(4):
            win = rows_in[pl.ds(pl.multiple_of(starts[n], ALIGN), seq), :]
            row = starts[n] + lax.broadcasted_iota(jnp.int32, win.shape, 0)
            valid = (row >= off[n]) & (row < off[n] + lens[n])
            wins[n] = jnp.where(valid, win.astype(F32), 0.0).astype(BF16)

    for j, part in enumerate(parts):
        held[j * u : (j + 1) * u, :] = part[0]
        k = 2 * pairs - 1 - j
        held[k * u : (k + 1) * u, :] = part[1]

    def add(n, skip, rows):
        at = pl.ds(pl.multiple_of(starts[n] + skip, ALIGN), rows)
        proj = lax.dot_general(
            held[at, :], wins[n, skip : skip + rows, :], (((0,), (0,)), ((), ())), preferred_element_type=F32
        )
        if n == 0:
            total[...] = proj * proj
        else:
            total[...] += proj * proj

    short = min(256, seq)
    for n in range(4):
        pl.when(al[n] <= short)(functools.partial(add, n, 0 if n < 2 else seq - short, short))
        pl.when(al[n] > short)(functools.partial(add, n, 0, seq))
    out_ref[...] = total[...].astype(out_ref.dtype)


def squares_of_pieces(cap, lens, me, side, parts, mine, other, seq, before=None):
    pairs = len(parts)
    u, cols = parts[0].shape[1:]
    ins = 2 * mine.shape[1]
    tile = TILE
    per = cols // tile
    at = lambda i, lens, me: ((me[0] % 2 ^ side) * per + i, 0)
    whole = pl.BlockSpec((cap, mine.shape[1]), lambda i, lens, me: (0, 0))
    extra = [] if before is None else [before]
    return pl.pallas_call(
        functools.partial(pieces_kernel, cap, pairs),
        grid_spec=pltpu.PrefetchScalarGridSpec(
            num_scalar_prefetch=2,
            grid=(per,),
            in_specs=[pl.BlockSpec((2, u, tile), lambda i, lens, me: (0, 0, i))] * pairs
            + [whole, whole]
            + [pl.BlockSpec(memory_space=pl.ANY)] * len(extra),
            out_specs=pl.BlockSpec((tile, ins), at),
            scratch_shapes=[
                pltpu.VMEM((cap, tile), BF16),
                pltpu.VMEM((cap, ins), BF16),
                pltpu.VMEM((4, seq, ins), BF16),
                pltpu.VMEM((tile, ins), F32),
            ],
        ),
        out_shape=jax.ShapeDtypeStruct((2 * cols, ins), BF16),
        input_output_aliases={} if before is None else {pairs + 4: 0},
        compiler_params=pltpu.CompilerParams(vmem_limit_bytes=36 * 2**20),
        cost_estimate=pl.CostEstimate(flops=1, bytes_accessed=1, transcendentals=0),
    )(lens, me.reshape(1), *parts, mine, other, *extra)


def swap_dp(x, k, n_dp):
    return lax.ppermute(x, "dp", [(d, d ^ k) for d in range(n_dp)])


def project_in(kept, blocks, me):
    rows = blocks[0].shape[0]
    total = None
    for k, b in enumerate(blocks):
        a = lax.dynamic_slice_in_dim(kept, (me ^ k) * rows, rows, axis=1)
        t = jnp.dot(a, b, preferred_element_type=F32)
        total = t if total is None else total + t
    return total.astype(BF16)


def mask_acts(acts, lengths):
    keep = (jnp.arange(acts.shape[1], dtype=jnp.int32)[None, :] < lengths[:, None]).astype(acts.dtype)
    return (acts * keep[:, :, None])[0]


def general(n_dp, acts, out_grads, basis_in, basis_out, lengths):
    seq = acts.shape[1]
    me = lax.axis_index("dp")
    kept = mask_acts(acts, lengths)

    def exchange(x, width):
        parts = [lax.dynamic_slice_in_dim(x, (me ^ k) * width, width, axis=1) for k in range(n_dp)]
        return [parts[0]] + [swap_dp(parts[k], k, n_dp) for k in range(1, n_dp)]

    far = swap_dp(basis_in, 2, n_dp)
    blocks = [basis_in, swap_dp(basis_in, 1, n_dp), far, swap_dp(far, 1, n_dp)]
    in_local = project_in(kept, blocks, me)
    n_chunks = 3
    step = seq // n_chunks
    outs = []
    for j in range(n_chunks):
        g = out_grads[0, j * step : (j + 1) * step]
        whole = lax.all_gather(g, "tensor", axis=1, tiled=True)
        mine = jnp.concatenate(exchange(whole, whole.shape[1] // n_dp), axis=0)
        part = jnp.dot(mine, basis_out, preferred_element_type=F32)
        part = part.reshape(n_dp, step, -1)
        odd = swap_dp(part[1::2].astype(BF16), 1, n_dp)
        s0 = part[0] + odd[0].astype(F32)
        s2 = part[2] + odd[1].astype(F32)
        far = swap_dp(jnp.stack([s2, s0]).astype(BF16), 2, n_dp)
        even = jnp.stack([s0 + far[0].astype(F32), s2 + far[1].astype(F32)]).astype(BF16)
        rest = swap_dp(even, 1, n_dp)
        outs.append(jnp.stack([even[0], rest[0], even[1], rest[1]]))
    in_all = lax.all_gather(in_local, "tensor", axis=1, tiled=True)
    in_proj = jnp.stack(exchange(in_all, in_all.shape[1] // n_dp))
    out_proj = jnp.concatenate(outs, axis=1).reshape(n_dp * seq, -1)
    return squares(jnp.arange(n_dp, dtype=jnp.int32) * seq, out_proj, in_proj)


def home_pairs(hops, across=False):
    pairs = []
    for x in (0, 1):
        for c in (0, 1):
            d = 2 * x + c
            for w0, w1 in hops:
                z0, z1 = (w0, w1) if x == 0 else (3 - w0, 3 - w1)
                if across:
                    pairs.append((z0 * 4 + (d ^ 2), z1 * 4 + d))
                else:
                    pairs.append((z0 * 4 + d, z1 * 4 + d))
    return pairs


def send(x, hops, across=False):
    return lax.ppermute(x, ("tensor", "dp"), home_pairs(hops, across))


def to_home(x):
    return send(x, [(0, 0), (1, 1)], True)


def tie(v, *after):
    return lax.optimization_barrier((v,) + after)[0]


def swap(v, k=1):
    return swap_dp(v, k, 4)


def compact(cap, acts, grads, following, basis_in, basis_out, lens):
    seq = acts.shape[1]
    me = lax.axis_index("dp")
    z = lax.axis_index("tensor")
    x, c = me // 2, me % 2
    w = jnp.where(x == 0, z, 3 - z)
    m = STEPS
    u = cap // m
    c2 = min(m, -(-min(2 * seq, cap - 2 * MIN_LEN) // u))
    want_outer = c == x
    kept = mask_acts(acts, lax.dynamic_slice_in_dim(lens, me, 1))

    def pack(a, b, split):
        return packs(cap, c2, split, lens, me, a, b)

    def merged(own, others, i):
        t = None
        if i < c2:
            t = own[i]
        if m - 1 - i < c2:
            o = others[m - 1 - i]
            t = o if t is None else t + o
        return t

    def halves(outer, inner):
        mine = jnp.where(want_outer, outer, inner)
        return mine, swap(jnp.where(want_outer, inner, outer))

    packed = pack(grads, following, True)
    arrived = [None] * c2
    last = None
    for i in range(c2 - 1, -1, -1):
        arrived[i] = to_home(packed[i] if last is None else tie(packed[i], last))
        last = arrived[i]
    far_in = swap(tie(basis_in, last), 2)
    near_in = swap(tie(basis_in, arrived[c2 - 1]))
    far_near = swap(far_in)

    blocks, given, held, sums, fars = ([None] * m for _ in range(5))
    own, fa, fb, m1 = [None] * m, [None] * (m + 1), [None] * m, [None] * m

    def meet(i):
        outer = jnp.where(w == 0, own[i], jnp.where(w == 1, fa[i], jnp.where(w == 2, fb[i], fa[i + 1])))
        inner = jnp.where(w == 0, m1[i], jnp.where(w == 1, own[i], jnp.where(w == 2, fa[i], fb[i])))
        blocks[i] = halves(outer, inner)

    def product(i):
        given[i], held[i] = products(c, *blocks[i], basis_out)

    def add_core(i):
        sums[i] = held[i] + swap(given[i]).astype(F32)
        fars[i] = swap(sums[i].astype(BF16), 2)

    in_local = None
    for i in range(m):
        own[i] = merged(packed, arrived, i)
        v = own[i] if i == 0 else jnp.where(w == 2, fb[i - 1], own[i])
        fa[i] = send(tie(v, *([held[i - 3]] if i >= 3 else [])), [(0, 1), (1, 2)] + ([(2, 3)] if i else []))
        m1[i] = send(own[i], [(1, 0)])
        if i >= 1:
            meet(i - 1)
        if i >= 3:
            add_core(i - 3)
        after = []
        if i >= 2:
            after += blocks[i - 2]
            product(i - 2)
        if i >= 3:
            after.append(sums[i - 3])
        if i == m - 1:
            in_local = project_in(kept, [basis_in, near_in, far_in, far_near], me)
            after.append(in_local)
        fb[i] = send(tie(fa[i], *after), [(1, 2), (2, 3)])

    hc = in_local.shape[1] // 2
    in_mine = lax.dynamic_slice_in_dim(in_local, c * hc, hc, axis=1)
    in_given = lax.dynamic_slice_in_dim(in_local, (1 - c) * hc, hc, axis=1)
    in_packed = pack(in_mine, swap(in_given), False)
    in_arrived = to_home(in_packed)
    in_own = jnp.concatenate([merged(in_packed, in_arrived, i) for i in range(m)], axis=0)

    after = [fb[m - 1], held[m - 3], fars[m - 4], blocks[m - 2][1]]
    fa[m] = send(tie(fb[m - 1], *after), [(2, 3)])
    r1 = send(tie(in_own, *after), [(0, 1), (1, 2)])
    i1 = send(in_own, [(1, 0)])
    add_core(m - 3)
    blocks[m - 2] = (tie(blocks[m - 2][0], fb[m - 1]), blocks[m - 2][1])
    product(m - 2)
    meet(m - 1)
    r2 = send(tie(r1, fa[m], sums[m - 3], held[m - 2]), [(1, 2), (2, 3)])
    add_core(m - 2)
    product(m - 1)
    r3 = send(tie(r2, fars[m - 3], sums[m - 2], held[m - 1]), [(2, 3)])
    add_core(m - 1)
    outer = jnp.where(w == 0, in_own, jnp.where(w == 1, r1, jnp.where(w == 2, r2, r3)))
    inner = jnp.where(w == 0, i1, jnp.where(w == 1, in_own, jnp.where(w == 2, r1, r2)))
    in_mine, in_other = halves(outer, inner)

    mine, rest = [None] * (m // 2), [None] * (m // 2)
    for j in range(m // 2 - 1, -1, -1):
        k = m - 1 - j
        late = tie(fars[k], in_mine, in_other) if j == 0 else fars[k]
        lo = jnp.where(x == 0, sums[j], sums[k]) + jnp.where(x == 0, late, fars[j]).astype(F32)
        hi = jnp.where(x == 0, sums[k], sums[j]) + jnp.where(x == 0, fars[j], late).astype(F32)
        mine[j] = jnp.stack([lo, hi]).astype(BF16)
        rest[j] = swap(mine[j])

    half = squares_of_pieces(cap, lens, me, 0, mine, in_mine, in_other, seq)
    return squares_of_pieces(cap, lens, me, 1, rest, in_mine, in_other, seq, half)


def special(caps, acts, out_grads, basis_in, basis_out, lengths):
    me = lax.axis_index("dp")
    c = me % 2
    every = lax.all_gather(lengths, ("groups", "dp"), axis=0, tiled=True)
    g = out_grads[0]
    half = g.shape[1] // 2
    mine = lax.dynamic_slice_in_dim(g, c * half, half, axis=1)
    given = lax.dynamic_slice_in_dim(g, (1 - c) * half, half, axis=1)
    following = swap_dp(given, 1, 4)
    totals = jnp.sum(((every + ALIGN - 1) // ALIGN * ALIGN).reshape(-1, 4), axis=1)
    need = jnp.max(totals)
    lens = lax.dynamic_slice_in_dim(every, lax.axis_index("groups") * 4, 4)
    index = jnp.int32(0)
    for cap in caps[:-1]:
        index = index + (need > cap).astype(jnp.int32)
    branches = [functools.partial(compact, cap) for cap in caps]
    return lax.switch(index, branches, acts, mine, following, basis_in, basis_out, lens)


def per_device(sizes, caps, acts, out_grads, basis_in, basis_out, lengths):
    if sizes == (4, 4):
        return special(caps, acts, out_grads, basis_in, basis_out, lengths)
    return general(sizes[1], acts, out_grads, basis_in, basis_out, lengths)


CAPS = (768, 832, 896, 960, 1152)


def solution(mesh):
    in_specs = (
        P(("groups", "dp"), None, None),
        P(("groups", "dp"), None, "tensor"),
        P(("groups", "dp"), "tensor"),
        P(("groups", "dp"), "tensor"),
        P(("groups", "dp")),
    )
    out_specs = P(("groups", "tensor"), "dp")
    sizes = (mesh.shape["tensor"], mesh.shape["dp"])
    return jax.shard_map(
        functools.partial(per_device, sizes, CAPS), mesh=mesh, in_specs=in_specs, out_specs=out_specs, check_vma=False
    )
```

```python
import functools

import jax
import jax.numpy as jnp
from jax import lax
from jax.experimental import pallas as pl
from jax.experimental.pallas import tpu as pltpu
from jax.sharding import PartitionSpec as P

F32 = jnp.float32
BF16 = jnp.bfloat16
MIN_LEN = 96
ALIGN = 16
TILE = 256
STEPS = 4


def square_kernel(start_ref, out_ref, in_ref, c_ref):
    total = None
    for n in range(in_ref.shape[0]):
        rows = pl.ds(pl.multiple_of(start_ref[n], ALIGN), in_ref.shape[1])
        proj = lax.dot_general(out_ref[rows, :], in_ref[n], (((0,), (0,)), ((), ())), preferred_element_type=F32)
        total = proj * proj if total is None else total + proj * proj
    c_ref[...] = total.astype(c_ref.dtype)


def squares(starts, out_proj, in_proj):
    tokens, cols = out_proj.shape
    n, seq, ins = in_proj.shape
    tile = cols
    for t in (512, 256, 128):
        if cols % t == 0:
            tile = t
            break
    return pl.pallas_call(
        square_kernel,
        grid_spec=pltpu.PrefetchScalarGridSpec(
            num_scalar_prefetch=1,
            grid=(cols // tile,),
            in_specs=[
                pl.BlockSpec((tokens, tile), lambda i, s: (0, i)),
                pl.BlockSpec((n, seq, ins), lambda i, s: (0, 0, 0)),
            ],
            out_specs=pl.BlockSpec((tile, ins), lambda i, s: (i, 0)),
        ),
        out_shape=jax.ShapeDtypeStruct((cols, ins), BF16),
        compiler_params=pltpu.CompilerParams(vmem_limit_bytes=60 * 2**20),
        cost_estimate=pl.CostEstimate(
            flops=2 * n * seq * cols * ins, bytes_accessed=2 * (n * seq * (cols + ins) + cols * ins), transcendentals=0
        ),
    )(starts, out_proj, in_proj)


def product_kernel(c_ref, mine_ref, other_ref, b_mine_ref, b_other_ref, given_ref, held_ref):
    i = pl.program_id(0)
    total = jnp.dot(mine_ref[...], b_mine_ref[...], preferred_element_type=F32)
    total = total + jnp.dot(other_ref[...], b_other_ref[...], preferred_element_type=F32)

    @pl.when(i < pl.num_programs(0) // 2)
    def _():
        given_ref[...] = total.astype(given_ref.dtype)

    @pl.when(i >= pl.num_programs(0) // 2)
    def _():
        held_ref[...] = total


def products(c, mine, other, basis):
    rows, depth = mine.shape
    cols = basis.shape[1] // 2
    tile = 896 if cols % 896 == 0 else TILE
    per = cols // tile
    at = lambda i, c: jnp.where(i < per, (1 - c[0]) * per + i, c[0] * per + i - per)
    return pl.pallas_call(
        product_kernel,
        grid_spec=pltpu.PrefetchScalarGridSpec(
            num_scalar_prefetch=1,
            grid=(2 * per,),
            in_specs=[
                pl.BlockSpec((rows, depth), lambda i, c: (0, 0)),
                pl.BlockSpec((rows, depth), lambda i, c: (0, 0)),
                pl.BlockSpec((depth, tile), lambda i, c: (c[0], at(i, c))),
                pl.BlockSpec((depth, tile), lambda i, c: (1 - c[0], at(i, c))),
            ],
            out_specs=[
                pl.BlockSpec((rows, tile), lambda i, c: (0, jnp.minimum(i, per - 1))),
                pl.BlockSpec((rows, tile), lambda i, c: (0, jnp.maximum(i - per, 0))),
            ],
        ),
        out_shape=[jax.ShapeDtypeStruct((rows, cols), BF16), jax.ShapeDtypeStruct((rows, cols), F32)],
        compiler_params=pltpu.CompilerParams(vmem_limit_bytes=36 * 2**20),
        cost_estimate=pl.CostEstimate(flops=1, bytes_accessed=1, transcendentals=0),
    )(c.reshape(1), mine, other, basis, basis)


def places(cap, lens):
    al = [(v + ALIGN - 1) // ALIGN * ALIGN for v in lens]
    return [jnp.int32(0), al[0], cap - al[3] - al[2], cap - al[3]], al


def choose(me, values):
    out = values[0]
    for k in range(1, len(values)):
        out = jnp.where(me == k, values[k], out)
    return out


def pack_kernel(cap, lens_ref, me_ref, own_ref, next_ref, *outs):
    me = me_ref[0]
    lens = [lens_ref[k] for k in range(4)]
    off = places(cap, lens)[0]
    seq = own_ref.shape[0]
    u = cap // STEPS
    for i in range(len(outs) if len(outs) > 1 else outs[0].shape[0]):
        first = jnp.where(me < 2, i, STEPS - 1 - i) * u
        row = first + lax.broadcasted_iota(jnp.int32, (u, seq), 0)
        s = lax.broadcasted_iota(jnp.int32, (u, seq), 1)
        total = None
        for n, ref in ((me, own_ref), (me ^ 1, next_ref)):
            hit = (row == s + choose(n, off)) & (s < choose(n, lens))
            t = jnp.dot(jnp.where(hit, 1.0, 0.0).astype(BF16), ref[...], preferred_element_type=F32)
            total = t if total is None else total + t
        if len(outs) > 1:
            outs[i][...] = total.astype(BF16)
        else:
            outs[0][i] = total.astype(BF16)


def packs(cap, count, split, lens, me, own, following):
    u, width = cap // STEPS, own.shape[1]
    if split and count > 1:
        shapes = [jax.ShapeDtypeStruct((u, width), BF16)] * count
    else:
        shapes = [jax.ShapeDtypeStruct((count, u, width), BF16)]
    out = pl.pallas_call(
        functools.partial(pack_kernel, cap),
        in_specs=[pl.BlockSpec(memory_space=pltpu.SMEM)] * 2 + [pl.BlockSpec(memory_space=pltpu.VMEM)] * 2,
        out_specs=[pl.BlockSpec(memory_space=pltpu.VMEM)] * len(shapes),
        out_shape=shapes,
        compiler_params=pltpu.CompilerParams(vmem_limit_bytes=24 * 2**20),
        cost_estimate=pl.CostEstimate(flops=1, bytes_accessed=1, transcendentals=0),
    )(lens, me.reshape(1), own, following)
    return out if split else out[0]


def pieces_kernel(cap, pairs, first, lens_ref, me_ref, *refs):
    parts = refs[:pairs]
    u = cap // STEPS
    lens = [lens_ref[k] for k in range(4)]
    off, al = places(cap, lens)
    if first:
        mine_ref, other_ref, out_ref, wins, held, rows_in = refs[pairs:]
    else:
        wins, _, out_ref, held = refs[pairs:]
    seq = wins.shape[1]
    starts = [off[0], off[1], off[2] + al[2] - seq, off[3] + al[3] - seq]

    if first:

        @pl.when(pl.program_id(0) == 0)
        def _():
            me = me_ref[0]
            c, hc = me % 2, mine_ref.shape[1]
            for p in range(STEPS):
                at = pl.ds(pl.multiple_of(jnp.where(me < 2, p, STEPS - 1 - p) * u, ALIGN), u)
                rows_in[at, pl.ds(pl.multiple_of(c * hc, 128), hc)] = mine_ref[p * u : (p + 1) * u, :]
                rows_in[at, pl.ds(pl.multiple_of((1 - c) * hc, 128), hc)] = other_ref[p * u : (p + 1) * u, :]
            for n in range(4):
                win = rows_in[pl.ds(pl.multiple_of(starts[n], ALIGN), seq), :]
                row = starts[n] + lax.broadcasted_iota(jnp.int32, win.shape, 0)
                valid = (row >= off[n]) & (row < off[n] + lens[n])
                wins[n] = jnp.where(valid, win.astype(F32), 0.0).astype(BF16)

    for j, part in enumerate(parts):
        held[j * u : (j + 1) * u, :] = part[0]
        k = 2 * pairs - 1 - j
        held[k * u : (k + 1) * u, :] = part[1]

    total = None
    for n in range(4):
        at = pl.ds(pl.multiple_of(starts[n], ALIGN), seq)
        proj = lax.dot_general(held[at, :], wins[n], (((0,), (0,)), ((), ())), preferred_element_type=F32)
        total = proj * proj if total is None else total + proj * proj
    out_ref[...] = total.astype(out_ref.dtype)


def squares_of_pieces(cap, lens, me, parts, in_halves, seq, before=None):
    first = before is None
    pairs = len(parts)
    u, cols = parts[0].shape[1:]
    ins = 2 * in_halves[0].shape[1] if first else before[0].shape[1]
    tile = TILE
    per = cols // tile
    side = 0 if first else 1
    at = lambda i, lens, me: ((me[0] % 2 ^ side) * per + i, 0)
    wins = pl.BlockSpec((4, seq, ins), lambda i, lens, me: (0, 0, 0))
    if first:
        more = [pl.BlockSpec((cap, ins // 2), lambda i, lens, me: (0, 0))] * 2
    else:
        more = [wins, pl.BlockSpec(memory_space=pl.ANY)]
        in_halves = [before[1], before[0]]
    result = jax.ShapeDtypeStruct((2 * cols, ins), BF16)
    out = pl.pallas_call(
        functools.partial(pieces_kernel, cap, pairs, first),
        grid_spec=pltpu.PrefetchScalarGridSpec(
            num_scalar_prefetch=2,
            grid=(per,),
            in_specs=[pl.BlockSpec((2, u, tile), lambda i, lens, me: (0, 0, i))] * pairs + more,
            out_specs=[pl.BlockSpec((tile, ins), at)] + ([wins] if first else []),
            scratch_shapes=[pltpu.VMEM((cap, tile), BF16)] + ([pltpu.VMEM((cap, ins), BF16)] if first else []),
        ),
        out_shape=[result] + ([jax.ShapeDtypeStruct((4, seq, ins), BF16)] if first else []),
        input_output_aliases={} if first else {pairs + 3: 0},
        compiler_params=pltpu.CompilerParams(vmem_limit_bytes=36 * 2**20),
        cost_estimate=pl.CostEstimate(flops=1, bytes_accessed=1, transcendentals=0),
    )(lens, me.reshape(1), *parts, *in_halves)
    return out if first else out[0]


def swap_dp(x, k, n_dp):
    return lax.ppermute(x, "dp", [(d, d ^ k) for d in range(n_dp)])


def project_in(kept, blocks, me):
    rows = blocks[0].shape[0]
    total = None
    for k, b in enumerate(blocks):
        a = lax.dynamic_slice_in_dim(kept, (me ^ k) * rows, rows, axis=1)
        t = jnp.dot(a, b, preferred_element_type=F32)
        total = t if total is None else total + t
    return total.astype(BF16)


def mask_acts(acts, lengths):
    keep = (jnp.arange(acts.shape[1], dtype=jnp.int32)[None, :] < lengths[:, None]).astype(acts.dtype)
    return (acts * keep[:, :, None])[0]


def general(n_dp, acts, out_grads, basis_in, basis_out, lengths):
    seq = acts.shape[1]
    me = lax.axis_index("dp")
    kept = mask_acts(acts, lengths)

    def exchange(x, width):
        parts = [lax.dynamic_slice_in_dim(x, (me ^ k) * width, width, axis=1) for k in range(n_dp)]
        return [parts[0]] + [swap_dp(parts[k], k, n_dp) for k in range(1, n_dp)]

    far = swap_dp(basis_in, 2, n_dp)
    blocks = [basis_in, swap_dp(basis_in, 1, n_dp), far, swap_dp(far, 1, n_dp)]
    in_local = project_in(kept, blocks, me)
    n_chunks = 3
    step = seq // n_chunks
    outs = []
    for j in range(n_chunks):
        g = out_grads[0, j * step : (j + 1) * step]
        whole = lax.all_gather(g, "tensor", axis=1, tiled=True)
        mine = jnp.concatenate(exchange(whole, whole.shape[1] // n_dp), axis=0)
        part = jnp.dot(mine, basis_out, preferred_element_type=F32)
        part = part.reshape(n_dp, step, -1)
        odd = swap_dp(part[1::2].astype(BF16), 1, n_dp)
        s0 = part[0] + odd[0].astype(F32)
        s2 = part[2] + odd[1].astype(F32)
        far = swap_dp(jnp.stack([s2, s0]).astype(BF16), 2, n_dp)
        even = jnp.stack([s0 + far[0].astype(F32), s2 + far[1].astype(F32)]).astype(BF16)
        rest = swap_dp(even, 1, n_dp)
        outs.append(jnp.stack([even[0], rest[0], even[1], rest[1]]))
    in_all = lax.all_gather(in_local, "tensor", axis=1, tiled=True)
    in_proj = jnp.stack(exchange(in_all, in_all.shape[1] // n_dp))
    out_proj = jnp.concatenate(outs, axis=1).reshape(n_dp * seq, -1)
    return squares(jnp.arange(n_dp, dtype=jnp.int32) * seq, out_proj, in_proj)


def home_pairs(hops, across=False):
    pairs = []
    for x in (0, 1):
        for c in (0, 1):
            d = 2 * x + c
            for w0, w1 in hops:
                z0, z1 = (w0, w1) if x == 0 else (3 - w0, 3 - w1)
                if across:
                    pairs.append((z0 * 4 + (d ^ 2), z1 * 4 + d))
                else:
                    pairs.append((z0 * 4 + d, z1 * 4 + d))
    return pairs


def send(x, hops, across=False):
    return lax.ppermute(x, ("tensor", "dp"), home_pairs(hops, across))


def to_home(x):
    return send(x, [(0, 0), (1, 1)], True)


def tie(v, *after):
    return lax.optimization_barrier((v,) + after)[0]


def swap(v, k=1):
    return swap_dp(v, k, 4)


def compact(cap, acts, grads, following, basis_in, basis_out, lens):
    seq = acts.shape[1]
    me = lax.axis_index("dp")
    z = lax.axis_index("tensor")
    x, c = me // 2, me % 2
    w = jnp.where(x == 0, z, 3 - z)
    m = STEPS
    u = cap // m
    c2 = min(m, -(-min(2 * seq, cap - 2 * MIN_LEN) // u))
    want_outer = c == x
    kept = mask_acts(acts, lax.dynamic_slice_in_dim(lens, me, 1))

    def pack(a, b, split):
        return packs(cap, c2, split, lens, me, a, b)

    def merged(own, others, i):
        t = None
        if i < c2:
            t = own[i]
        if m - 1 - i < c2:
            o = others[m - 1 - i]
            t = o if t is None else t + o
        return t

    def halves(outer, inner):
        mine = jnp.where(want_outer, outer, inner)
        return mine, swap(jnp.where(want_outer, inner, outer))

    packed = pack(grads, following, True)
    arrived = [None] * c2
    for i in range(c2 - 1, -1, -1):
        arrived[i] = to_home(packed[i] if i >= c2 - 2 else tie(packed[i], arrived[c2 - 1]))
    far_in = swap(tie(basis_in, arrived[c2 - 1]), 2)
    near_in = swap(tie(basis_in, arrived[c2 - 1]))
    far_near = swap(far_in)

    blocks, given, held, sums, fars = ([None] * m for _ in range(5))
    own, fa, fb, m1 = [None] * m, [None] * (m + 1), [None] * m, [None] * m

    def meet(i):
        outer = jnp.where(w == 0, own[i], jnp.where(w == 1, fa[i], jnp.where(w == 2, fb[i], fa[i + 1])))
        inner = jnp.where(w == 0, m1[i], jnp.where(w == 1, own[i], jnp.where(w == 2, fa[i], fb[i])))
        blocks[i] = halves(outer, inner)

    def product(i):
        mine, other = blocks[i]
        if i >= 1:
            mine = tie(mine, sums[i - 1])
        given[i], held[i] = products(c, mine, other, basis_out)

    def add_core(i):
        sums[i] = held[i] + swap(given[i]).astype(F32)
        fars[i] = swap(sums[i].astype(BF16), 2)

    in_local = None
    for i in range(m):
        own[i] = merged(packed, arrived, i)
        v = own[i] if i == 0 else jnp.where(w == 2, fb[i - 1], own[i])
        after = []
        if i >= 2:
            after += blocks[i - 2]
        if i >= 3:
            after.append(sums[i - 3])
        fa[i] = send(tie(v, *after), [(0, 1), (1, 2)] + ([(2, 3)] if i else []))
        m1[i] = send(own[i], [(1, 0)])
        if i >= 2:
            blocks[i - 2] = (tie(blocks[i - 2][0], fb[i - 1]), blocks[i - 2][1])
            product(i - 2)
            add_core(i - 2)
        if i >= 1:
            meet(i - 1)
        after = []
        if i >= 2:
            after.append(held[i - 2])
        if i >= 3:
            after.append(fars[i - 3])
        if i == m - 1:
            in_local = project_in(kept, [basis_in, near_in, far_in, far_near], me)
            after.append(in_local)
        fb[i] = send(tie(fa[i], *after), [(1, 2), (2, 3)])

    hc = in_local.shape[1] // 2
    in_mine = lax.dynamic_slice_in_dim(in_local, c * hc, hc, axis=1)
    in_given = lax.dynamic_slice_in_dim(in_local, (1 - c) * hc, hc, axis=1)
    in_packed = pack(in_mine, swap(in_given), False)
    in_arrived = to_home(in_packed)
    in_own = jnp.concatenate([merged(in_packed, in_arrived, i) for i in range(m)], axis=0)

    after = [fb[m - 1], sums[m - 3], blocks[m - 2][1]]
    fa[m] = send(tie(fb[m - 1], *after), [(2, 3)])
    r1 = send(tie(in_own, *after), [(0, 1), (1, 2)])
    i1 = send(in_own, [(1, 0)])
    blocks[m - 2] = (tie(blocks[m - 2][0], fb[m - 1]), blocks[m - 2][1])
    product(m - 2)
    add_core(m - 2)
    meet(m - 1)
    r2 = send(tie(r1, fa[m], fars[m - 3], held[m - 2]), [(1, 2), (2, 3)])
    product(m - 1)
    r3 = send(tie(r2, fars[m - 2], held[m - 1]), [(2, 3)])
    add_core(m - 1)
    outer = jnp.where(w == 0, in_own, jnp.where(w == 1, r1, jnp.where(w == 2, r2, r3)))
    inner = jnp.where(w == 0, i1, jnp.where(w == 1, in_own, jnp.where(w == 2, r1, r2)))
    in_mine, in_other = halves(outer, inner)

    mine, rest = [None] * (m // 2), [None] * (m // 2)
    for j in range(m // 2 - 1, -1, -1):
        k = m - 1 - j
        late = tie(fars[k], in_mine, in_other) if j == 0 else fars[k]
        lo = jnp.where(x == 0, sums[j], sums[k]) + jnp.where(x == 0, late, fars[j]).astype(F32)
        hi = jnp.where(x == 0, sums[k], sums[j]) + jnp.where(x == 0, fars[j], late).astype(F32)
        mine[j] = jnp.stack([lo, hi]).astype(BF16)
        rest[j] = swap(mine[j])

    half = squares_of_pieces(cap, lens, me, mine, [in_mine, in_other], seq)
    return squares_of_pieces(cap, lens, me, rest, None, seq, half)


def special(caps, acts, out_grads, basis_in, basis_out, lengths):
    me = lax.axis_index("dp")
    c = me % 2
    every = lax.all_gather(lengths, ("groups", "dp"), axis=0, tiled=True)
    g = out_grads[0]
    half = g.shape[1] // 2
    mine = lax.dynamic_slice_in_dim(g, c * half, half, axis=1)
    given = lax.dynamic_slice_in_dim(g, (1 - c) * half, half, axis=1)
    following = swap_dp(given, 1, 4)
    totals = jnp.sum(((every + ALIGN - 1) // ALIGN * ALIGN).reshape(-1, 4), axis=1)
    need = jnp.max(totals)
    lens = lax.dynamic_slice_in_dim(every, lax.axis_index("groups") * 4, 4)
    index = jnp.int32(0)
    for cap in caps[:-1]:
        index = index + (need > cap).astype(jnp.int32)
    branches = [functools.partial(compact, cap) for cap in caps]
    return lax.switch(index, branches, acts, mine, following, basis_in, basis_out, lens)


def per_device(sizes, caps, acts, out_grads, basis_in, basis_out, lengths):
    if sizes == (4, 4):
        return special(caps, acts, out_grads, basis_in, basis_out, lengths)
    return general(sizes[1], acts, out_grads, basis_in, basis_out, lengths)


CAPS = (768, 832, 896, 960, 1152)


def solution(mesh):
    in_specs = (
        P(("groups", "dp"), None, None),
        P(("groups", "dp"), None, "tensor"),
        P(("groups", "dp"), "tensor"),
        P(("groups", "dp"), "tensor"),
        P(("groups", "dp")),
    )
    out_specs = P(("groups", "tensor"), "dp")
    sizes = (mesh.shape["tensor"], mesh.shape["dp"])
    return jax.shard_map(
        functools.partial(per_device, sizes, CAPS), mesh=mesh, in_specs=in_specs, out_specs=out_specs, check_vma=False
    )
```

```python
import functools

import jax
import jax.numpy as jnp
from jax import lax
from jax.experimental import pallas as pl
from jax.experimental.pallas import tpu as pltpu
from jax.sharding import PartitionSpec as P

F32 = jnp.float32
BF16 = jnp.bfloat16
MIN_LEN = 96
ALIGN = 16
TILE = 256
STEPS = 4


def square_kernel(start_ref, out_ref, in_ref, c_ref):
    total = None
    for n in range(in_ref.shape[0]):
        rows = pl.ds(pl.multiple_of(start_ref[n], ALIGN), in_ref.shape[1])
        proj = lax.dot_general(out_ref[rows, :], in_ref[n], (((0,), (0,)), ((), ())), preferred_element_type=F32)
        total = proj * proj if total is None else total + proj * proj
    c_ref[...] = total.astype(c_ref.dtype)


def squares(starts, out_proj, in_proj):
    tokens, cols = out_proj.shape
    n, seq, ins = in_proj.shape
    tile = cols
    for t in (512, 256, 128):
        if cols % t == 0:
            tile = t
            break
    return pl.pallas_call(
        square_kernel,
        grid_spec=pltpu.PrefetchScalarGridSpec(
            num_scalar_prefetch=1,
            grid=(cols // tile,),
            in_specs=[
                pl.BlockSpec((tokens, tile), lambda i, s: (0, i)),
                pl.BlockSpec((n, seq, ins), lambda i, s: (0, 0, 0)),
            ],
            out_specs=pl.BlockSpec((tile, ins), lambda i, s: (i, 0)),
        ),
        out_shape=jax.ShapeDtypeStruct((cols, ins), BF16),
        compiler_params=pltpu.CompilerParams(vmem_limit_bytes=60 * 2**20),
        cost_estimate=pl.CostEstimate(
            flops=2 * n * seq * cols * ins, bytes_accessed=2 * (n * seq * (cols + ins) + cols * ins), transcendentals=0
        ),
    )(starts, out_proj, in_proj)


def product_kernel(c_ref, mine_ref, other_ref, b_mine_ref, b_other_ref, given_ref, held_ref):
    i = pl.program_id(0)
    total = jnp.dot(mine_ref[...], b_mine_ref[...], preferred_element_type=F32)
    total = total + jnp.dot(other_ref[...], b_other_ref[...], preferred_element_type=F32)

    @pl.when(i < pl.num_programs(0) // 2)
    def _():
        given_ref[...] = total.astype(given_ref.dtype)

    @pl.when(i >= pl.num_programs(0) // 2)
    def _():
        held_ref[...] = total


def products(c, mine, other, basis):
    rows, depth = mine.shape
    cols = basis.shape[1] // 2
    tile = 896 if cols % 896 == 0 else TILE
    per = cols // tile
    at = lambda i, c: jnp.where(i < per, (1 - c[0]) * per + i, c[0] * per + i - per)
    return pl.pallas_call(
        product_kernel,
        grid_spec=pltpu.PrefetchScalarGridSpec(
            num_scalar_prefetch=1,
            grid=(2 * per,),
            in_specs=[
                pl.BlockSpec((rows, depth), lambda i, c: (0, 0)),
                pl.BlockSpec((rows, depth), lambda i, c: (0, 0)),
                pl.BlockSpec((depth, tile), lambda i, c: (c[0], at(i, c))),
                pl.BlockSpec((depth, tile), lambda i, c: (1 - c[0], at(i, c))),
            ],
            out_specs=[
                pl.BlockSpec((rows, tile), lambda i, c: (0, jnp.minimum(i, per - 1))),
                pl.BlockSpec((rows, tile), lambda i, c: (0, jnp.maximum(i - per, 0))),
            ],
        ),
        out_shape=[jax.ShapeDtypeStruct((rows, cols), BF16), jax.ShapeDtypeStruct((rows, cols), F32)],
        compiler_params=pltpu.CompilerParams(vmem_limit_bytes=36 * 2**20),
        cost_estimate=pl.CostEstimate(flops=1, bytes_accessed=1, transcendentals=0),
    )(c.reshape(1), mine, other, basis, basis)


def places(cap, lens):
    al = [(v + ALIGN - 1) // ALIGN * ALIGN for v in lens]
    return [jnp.int32(0), al[0], cap - al[3] - al[2], cap - al[3]], al


def choose(me, values):
    out = values[0]
    for k in range(1, len(values)):
        out = jnp.where(me == k, values[k], out)
    return out


def pack_kernel(cap, lens_ref, me_ref, own_ref, next_ref, *outs):
    me = me_ref[0]
    lens = [lens_ref[k] for k in range(4)]
    off = places(cap, lens)[0]
    seq = own_ref.shape[0]
    u = cap // STEPS
    for i in range(len(outs) if len(outs) > 1 else outs[0].shape[0]):
        first = jnp.where(me < 2, i, STEPS - 1 - i) * u
        row = first + lax.broadcasted_iota(jnp.int32, (u, seq), 0)
        s = lax.broadcasted_iota(jnp.int32, (u, seq), 1)
        total = None
        for n, ref in ((me, own_ref), (me ^ 1, next_ref)):
            hit = (row == s + choose(n, off)) & (s < choose(n, lens))
            t = jnp.dot(jnp.where(hit, 1.0, 0.0).astype(BF16), ref[...], preferred_element_type=F32)
            total = t if total is None else total + t
        if len(outs) > 1:
            outs[i][...] = total.astype(BF16)
        else:
            outs[0][i] = total.astype(BF16)


def packs(cap, count, split, lens, me, own, following):
    u, width = cap // STEPS, own.shape[1]
    if split and count > 1:
        shapes = [jax.ShapeDtypeStruct((u, width), BF16)] * count
    else:
        shapes = [jax.ShapeDtypeStruct((count, u, width), BF16)]
    out = pl.pallas_call(
        functools.partial(pack_kernel, cap),
        in_specs=[pl.BlockSpec(memory_space=pltpu.SMEM)] * 2 + [pl.BlockSpec(memory_space=pltpu.VMEM)] * 2,
        out_specs=[pl.BlockSpec(memory_space=pltpu.VMEM)] * len(shapes),
        out_shape=shapes,
        compiler_params=pltpu.CompilerParams(vmem_limit_bytes=24 * 2**20),
        cost_estimate=pl.CostEstimate(flops=1, bytes_accessed=1, transcendentals=0),
    )(lens, me.reshape(1), own, following)
    return out if split else out[0]


def pieces_kernel(cap, pairs, first, lens_ref, me_ref, *refs):
    parts = refs[:pairs]
    u = cap // STEPS
    lens = [lens_ref[k] for k in range(4)]
    off, al = places(cap, lens)
    if first:
        mine_ref, other_ref, out_ref, wins, held, rows_in = refs[pairs:]
    else:
        wins, _, out_ref, held = refs[pairs:]
    seq = wins.shape[1]
    starts = [off[0], off[1], off[2] + al[2] - seq, off[3] + al[3] - seq]

    if first:

        @pl.when(pl.program_id(0) == 0)
        def _():
            me = me_ref[0]
            c, hc = me % 2, mine_ref.shape[1]
            for p in range(STEPS):
                at = pl.ds(pl.multiple_of(jnp.where(me < 2, p, STEPS - 1 - p) * u, ALIGN), u)
                rows_in[at, pl.ds(pl.multiple_of(c * hc, 128), hc)] = mine_ref[p * u : (p + 1) * u, :]
                rows_in[at, pl.ds(pl.multiple_of((1 - c) * hc, 128), hc)] = other_ref[p * u : (p + 1) * u, :]
            for n in range(4):
                win = rows_in[pl.ds(pl.multiple_of(starts[n], ALIGN), seq), :]
                row = starts[n] + lax.broadcasted_iota(jnp.int32, win.shape, 0)
                valid = (row >= off[n]) & (row < off[n] + lens[n])
                wins[n] = jnp.where(valid, win.astype(F32), 0.0).astype(BF16)

    for j, part in enumerate(parts):
        held[j * u : (j + 1) * u, :] = part[0]
        k = 2 * pairs - 1 - j
        held[k * u : (k + 1) * u, :] = part[1]

    total = None
    for n in range(4):
        at = pl.ds(pl.multiple_of(starts[n], ALIGN), seq)
        proj = lax.dot_general(held[at, :], wins[n], (((0,), (0,)), ((), ())), preferred_element_type=F32)
        total = proj * proj if total is None else total + proj * proj
    out_ref[...] = total.astype(out_ref.dtype)


def squares_of_pieces(cap, lens, me, parts, in_halves, seq, before=None):
    first = before is None
    pairs = len(parts)
    u, cols = parts[0].shape[1:]
    ins = 2 * in_halves[0].shape[1] if first else before[0].shape[1]
    tile = TILE
    per = cols // tile
    side = 0 if first else 1
    at = lambda i, lens, me: ((me[0] % 2 ^ side) * per + i, 0)
    wins = pl.BlockSpec((4, seq, ins), lambda i, lens, me: (0, 0, 0))
    if first:
        more = [pl.BlockSpec((cap, ins // 2), lambda i, lens, me: (0, 0))] * 2
    else:
        more = [wins, pl.BlockSpec(memory_space=pl.ANY)]
        in_halves = [before[1], before[0]]
    result = jax.ShapeDtypeStruct((2 * cols, ins), BF16)
    out = pl.pallas_call(
        functools.partial(pieces_kernel, cap, pairs, first),
        grid_spec=pltpu.PrefetchScalarGridSpec(
            num_scalar_prefetch=2,
            grid=(per,),
            in_specs=[pl.BlockSpec((2, u, tile), lambda i, lens, me: (0, 0, i))] * pairs + more,
            out_specs=[pl.BlockSpec((tile, ins), at)] + ([wins] if first else []),
            scratch_shapes=[pltpu.VMEM((cap, tile), BF16)] + ([pltpu.VMEM((cap, ins), BF16)] if first else []),
        ),
        out_shape=[result] + ([jax.ShapeDtypeStruct((4, seq, ins), BF16)] if first else []),
        input_output_aliases={} if first else {pairs + 3: 0},
        compiler_params=pltpu.CompilerParams(vmem_limit_bytes=36 * 2**20),
        cost_estimate=pl.CostEstimate(flops=1, bytes_accessed=1, transcendentals=0),
    )(lens, me.reshape(1), *parts, *in_halves)
    return out if first else out[0]


def swap_dp(x, k, n_dp):
    return lax.ppermute(x, "dp", [(d, d ^ k) for d in range(n_dp)])


def project_in(kept, blocks, me):
    rows = blocks[0].shape[0]
    total = None
    for k, b in enumerate(blocks):
        a = lax.dynamic_slice_in_dim(kept, (me ^ k) * rows, rows, axis=1)
        t = jnp.dot(a, b, preferred_element_type=F32)
        total = t if total is None else total + t
    return total.astype(BF16)


def mask_acts(acts, lengths):
    keep = (jnp.arange(acts.shape[1], dtype=jnp.int32)[None, :] < lengths[:, None]).astype(acts.dtype)
    return (acts * keep[:, :, None])[0]


def general(n_dp, acts, out_grads, basis_in, basis_out, lengths):
    seq = acts.shape[1]
    me = lax.axis_index("dp")
    kept = mask_acts(acts, lengths)

    def exchange(x, width):
        parts = [lax.dynamic_slice_in_dim(x, (me ^ k) * width, width, axis=1) for k in range(n_dp)]
        return [parts[0]] + [swap_dp(parts[k], k, n_dp) for k in range(1, n_dp)]

    far = swap_dp(basis_in, 2, n_dp)
    blocks = [basis_in, swap_dp(basis_in, 1, n_dp), far, swap_dp(far, 1, n_dp)]
    in_local = project_in(kept, blocks, me)
    n_chunks = 3
    step = seq // n_chunks
    outs = []
    for j in range(n_chunks):
        g = out_grads[0, j * step : (j + 1) * step]
        whole = lax.all_gather(g, "tensor", axis=1, tiled=True)
        mine = jnp.concatenate(exchange(whole, whole.shape[1] // n_dp), axis=0)
        part = jnp.dot(mine, basis_out, preferred_element_type=F32)
        part = part.reshape(n_dp, step, -1)
        odd = swap_dp(part[1::2].astype(BF16), 1, n_dp)
        s0 = part[0] + odd[0].astype(F32)
        s2 = part[2] + odd[1].astype(F32)
        far = swap_dp(jnp.stack([s2, s0]).astype(BF16), 2, n_dp)
        even = jnp.stack([s0 + far[0].astype(F32), s2 + far[1].astype(F32)]).astype(BF16)
        rest = swap_dp(even, 1, n_dp)
        outs.append(jnp.stack([even[0], rest[0], even[1], rest[1]]))
    in_all = lax.all_gather(in_local, "tensor", axis=1, tiled=True)
    in_proj = jnp.stack(exchange(in_all, in_all.shape[1] // n_dp))
    out_proj = jnp.concatenate(outs, axis=1).reshape(n_dp * seq, -1)
    return squares(jnp.arange(n_dp, dtype=jnp.int32) * seq, out_proj, in_proj)


def home_pairs(hops, across=False):
    pairs = []
    for x in (0, 1):
        for c in (0, 1):
            d = 2 * x + c
            for w0, w1 in hops:
                z0, z1 = (w0, w1) if x == 0 else (3 - w0, 3 - w1)
                if across:
                    pairs.append((z0 * 4 + (d ^ 2), z1 * 4 + d))
                else:
                    pairs.append((z0 * 4 + d, z1 * 4 + d))
    return pairs


def send(x, hops, across=False):
    return lax.ppermute(x, ("tensor", "dp"), home_pairs(hops, across))


def to_home(x):
    return send(x, [(0, 0), (1, 1)], True)


def tie(v, *after):
    return lax.optimization_barrier((v,) + after)[0]


def swap(v, k=1):
    return swap_dp(v, k, 4)


def compact(cap, acts, grads, following, basis_in, basis_out, lens):
    seq = acts.shape[1]
    me = lax.axis_index("dp")
    z = lax.axis_index("tensor")
    x, c = me // 2, me % 2
    w = jnp.where(x == 0, z, 3 - z)
    m = STEPS
    u = cap // m
    c2 = min(m, -(-min(2 * seq, cap - 2 * MIN_LEN) // u))
    want_outer = c == x
    kept = mask_acts(acts, lax.dynamic_slice_in_dim(lens, me, 1))

    def pack(a, b, split):
        return packs(cap, c2, split, lens, me, a, b)

    def merged(own, others, i):
        t = None
        if i < c2:
            t = own[i]
        if m - 1 - i < c2:
            o = others[m - 1 - i]
            t = o if t is None else t + o
        return t

    def halves(outer, inner):
        mine = jnp.where(want_outer, outer, inner)
        return mine, swap(jnp.where(want_outer, inner, outer))

    packed = pack(grads, following, True)
    arrived = [None] * c2
    for i in range(c2 - 1, -1, -1):
        arrived[i] = to_home(packed[i] if i >= c2 - 2 else tie(packed[i], arrived[c2 - 1]))
    far_in = swap(tie(basis_in, arrived[c2 - 1]), 2)
    near_in = swap(tie(basis_in, arrived[c2 - 1]))

    blocks, given, held, sums, fars = ([None] * m for _ in range(5))
    own, fa, fb, m1 = [None] * m, [None] * (m + 1), [None] * m, [None] * m

    def meet(i):
        outer = jnp.where(w == 0, own[i], jnp.where(w == 1, fa[i], jnp.where(w == 2, fb[i], fa[i + 1])))
        inner = jnp.where(w == 0, m1[i], jnp.where(w == 1, own[i], jnp.where(w == 2, fa[i], fb[i])))
        blocks[i] = halves(outer, inner)

    def product(i):
        mine, other = blocks[i]
        if i >= 1:
            mine = tie(mine, sums[i - 1])
        given[i], held[i] = products(c, mine, other, basis_out)

    def add_core(i):
        sums[i] = held[i] + swap(given[i]).astype(F32)
        fars[i] = swap(sums[i].astype(BF16), 2)

    in_local = None
    for i in range(m):
        own[i] = merged(packed, arrived, i)
        v = own[i] if i == 0 else jnp.where(w == 2, fb[i - 1], own[i])
        after = []
        if i >= 2:
            after += blocks[i - 2]
        if i >= 3:
            after.append(sums[i - 3])
        fa[i] = send(tie(v, *after), [(0, 1), (1, 2)] + ([(2, 3)] if i else []))
        m1[i] = send(own[i], [(1, 0)])
        if i >= 2:
            blocks[i - 2] = (tie(blocks[i - 2][0], fb[i - 1]), blocks[i - 2][1])
            product(i - 2)
            add_core(i - 2)
        if i >= 1:
            meet(i - 1)
        after = []
        if i >= 2:
            after.append(held[i - 2])
        if i >= 3:
            after.append(fars[i - 3])
        if i == m - 1:
            far_in = tie(far_in, fb[i - 1])
            far_near = swap(far_in)
            in_local = project_in(kept, [basis_in, near_in, far_in, far_near], me)
            after.append(in_local)
        fb[i] = send(tie(fa[i], *after), [(1, 2), (2, 3)])

    hc = in_local.shape[1] // 2
    in_mine = lax.dynamic_slice_in_dim(in_local, c * hc, hc, axis=1)
    in_given = lax.dynamic_slice_in_dim(in_local, (1 - c) * hc, hc, axis=1)
    in_packed = pack(in_mine, swap(in_given), False)
    in_arrived = to_home(in_packed)
    in_own = jnp.concatenate([merged(in_packed, in_arrived, i) for i in range(m)], axis=0)

    after = [fb[m - 1], sums[m - 3], blocks[m - 2][1]]
    fa[m] = send(tie(fb[m - 1], *after), [(2, 3)])
    r1 = send(tie(in_own, *after), [(0, 1), (1, 2)])
    i1 = send(in_own, [(1, 0)])
    blocks[m - 2] = (tie(blocks[m - 2][0], fb[m - 1]), blocks[m - 2][1])
    product(m - 2)
    add_core(m - 2)
    meet(m - 1)
    r2 = send(tie(r1, fa[m], fars[m - 3], held[m - 2]), [(1, 2), (2, 3)])
    product(m - 1)
    r3 = send(tie(r2, fars[m - 2], held[m - 1]), [(2, 3)])
    add_core(m - 1)
    outer = jnp.where(w == 0, in_own, jnp.where(w == 1, r1, jnp.where(w == 2, r2, r3)))
    inner = jnp.where(w == 0, i1, jnp.where(w == 1, in_own, jnp.where(w == 2, r1, r2)))
    in_mine, in_other = halves(outer, inner)

    mine, rest = [None] * (m // 2), [None] * (m // 2)
    for j in range(m // 2 - 1, -1, -1):
        k = m - 1 - j
        late = tie(fars[k], in_mine, in_other) if j == 0 else fars[k]
        lo = jnp.where(x == 0, sums[j], sums[k]) + jnp.where(x == 0, late, fars[j]).astype(F32)
        hi = jnp.where(x == 0, sums[k], sums[j]) + jnp.where(x == 0, fars[j], late).astype(F32)
        mine[j] = jnp.stack([lo, hi]).astype(BF16)
        rest[j] = swap(mine[j])

    half = squares_of_pieces(cap, lens, me, mine, [in_mine, in_other], seq)
    return squares_of_pieces(cap, lens, me, rest, None, seq, half)


def special(caps, acts, out_grads, basis_in, basis_out, lengths):
    me = lax.axis_index("dp")
    c = me % 2
    every = lax.all_gather(lengths, ("groups", "dp"), axis=0, tiled=True)
    g = out_grads[0]
    half = g.shape[1] // 2
    mine = lax.dynamic_slice_in_dim(g, c * half, half, axis=1)
    given = lax.dynamic_slice_in_dim(g, (1 - c) * half, half, axis=1)
    following = swap_dp(given, 1, 4)
    totals = jnp.sum(((every + ALIGN - 1) // ALIGN * ALIGN).reshape(-1, 4), axis=1)
    need = jnp.max(totals)
    lens = lax.dynamic_slice_in_dim(every, lax.axis_index("groups") * 4, 4)
    index = jnp.int32(0)
    for cap in caps[:-1]:
        index = index + (need > cap).astype(jnp.int32)
    branches = [functools.partial(compact, cap) for cap in caps]
    return lax.switch(index, branches, acts, mine, following, basis_in, basis_out, lens)


def per_device(sizes, caps, acts, out_grads, basis_in, basis_out, lengths):
    if sizes == (4, 4):
        return special(caps, acts, out_grads, basis_in, basis_out, lengths)
    return general(sizes[1], acts, out_grads, basis_in, basis_out, lengths)


CAPS = (768, 832, 896, 960, 1152)


def solution(mesh):
    in_specs = (
        P(("groups", "dp"), None, None),
        P(("groups", "dp"), None, "tensor"),
        P(("groups", "dp"), "tensor"),
        P(("groups", "dp"), "tensor"),
        P(("groups", "dp")),
    )
    out_specs = P(("groups", "tensor"), "dp")
    sizes = (mesh.shape["tensor"], mesh.shape["dp"])
    return jax.shard_map(
        functools.partial(per_device, sizes, CAPS), mesh=mesh, in_specs=in_specs, out_specs=out_specs, check_vma=False
    )
```

```python
import functools

import jax
import jax.numpy as jnp
from jax import lax
from jax.experimental import pallas as pl
from jax.experimental.pallas import tpu as pltpu
from jax.sharding import PartitionSpec as P

F32 = jnp.float32
BF16 = jnp.bfloat16
MIN_LEN = 96
ALIGN = 16
TILE = 256
STEPS = 4


def square_kernel(start_ref, out_ref, in_ref, c_ref):
    total = None
    for n in range(in_ref.shape[0]):
        rows = pl.ds(pl.multiple_of(start_ref[n], ALIGN), in_ref.shape[1])
        proj = lax.dot_general(out_ref[rows, :], in_ref[n], (((0,), (0,)), ((), ())), preferred_element_type=F32)
        total = proj * proj if total is None else total + proj * proj
    c_ref[...] = total.astype(c_ref.dtype)


def squares(starts, out_proj, in_proj):
    tokens, cols = out_proj.shape
    n, seq, ins = in_proj.shape
    tile = cols
    for t in (512, 256, 128):
        if cols % t == 0:
            tile = t
            break
    return pl.pallas_call(
        square_kernel,
        grid_spec=pltpu.PrefetchScalarGridSpec(
            num_scalar_prefetch=1,
            grid=(cols // tile,),
            in_specs=[
                pl.BlockSpec((tokens, tile), lambda i, s: (0, i)),
                pl.BlockSpec((n, seq, ins), lambda i, s: (0, 0, 0)),
            ],
            out_specs=pl.BlockSpec((tile, ins), lambda i, s: (i, 0)),
        ),
        out_shape=jax.ShapeDtypeStruct((cols, ins), BF16),
        compiler_params=pltpu.CompilerParams(vmem_limit_bytes=60 * 2**20),
        cost_estimate=pl.CostEstimate(
            flops=2 * n * seq * cols * ins, bytes_accessed=2 * (n * seq * (cols + ins) + cols * ins), transcendentals=0
        ),
    )(starts, out_proj, in_proj)


def product_kernel(c_ref, mine_ref, other_ref, b_mine_ref, b_other_ref, given_ref, held_ref):
    i = pl.program_id(0)
    total = jnp.dot(mine_ref[...], b_mine_ref[...], preferred_element_type=F32)
    total = total + jnp.dot(other_ref[...], b_other_ref[...], preferred_element_type=F32)

    @pl.when(i < pl.num_programs(0) // 2)
    def _():
        given_ref[...] = total.astype(given_ref.dtype)

    @pl.when(i >= pl.num_programs(0) // 2)
    def _():
        held_ref[...] = total


def products(c, mine, other, basis):
    rows, depth = mine.shape
    cols = basis.shape[1] // 2
    tile = 896 if cols % 896 == 0 else TILE
    per = cols // tile
    at = lambda i, c: jnp.where(i < per, (1 - c[0]) * per + i, c[0] * per + i - per)
    return pl.pallas_call(
        product_kernel,
        grid_spec=pltpu.PrefetchScalarGridSpec(
            num_scalar_prefetch=1,
            grid=(2 * per,),
            in_specs=[
                pl.BlockSpec((rows, depth), lambda i, c: (0, 0)),
                pl.BlockSpec((rows, depth), lambda i, c: (0, 0)),
                pl.BlockSpec((depth, tile), lambda i, c: (c[0], at(i, c))),
                pl.BlockSpec((depth, tile), lambda i, c: (1 - c[0], at(i, c))),
            ],
            out_specs=[
                pl.BlockSpec((rows, tile), lambda i, c: (0, jnp.minimum(i, per - 1))),
                pl.BlockSpec((rows, tile), lambda i, c: (0, jnp.maximum(i - per, 0))),
            ],
        ),
        out_shape=[jax.ShapeDtypeStruct((rows, cols), BF16), jax.ShapeDtypeStruct((rows, cols), F32)],
        compiler_params=pltpu.CompilerParams(vmem_limit_bytes=36 * 2**20),
        cost_estimate=pl.CostEstimate(flops=1, bytes_accessed=1, transcendentals=0),
    )(c.reshape(1), mine, other, basis, basis)


def places(cap, lens):
    al = [(v + ALIGN - 1) // ALIGN * ALIGN for v in lens]
    return [jnp.int32(0), al[0], cap - al[3] - al[2], cap - al[3]], al


def choose(me, values):
    out = values[0]
    for k in range(1, len(values)):
        out = jnp.where(me == k, values[k], out)
    return out


def pack_kernel(cap, lens_ref, me_ref, own_ref, next_ref, *outs):
    me = me_ref[0]
    lens = [lens_ref[k] for k in range(4)]
    off = places(cap, lens)[0]
    seq = own_ref.shape[0]
    u = cap // STEPS
    for i in range(len(outs) if len(outs) > 1 else outs[0].shape[0]):
        first = jnp.where(me < 2, i, STEPS - 1 - i) * u
        row = first + lax.broadcasted_iota(jnp.int32, (u, seq), 0)
        s = lax.broadcasted_iota(jnp.int32, (u, seq), 1)
        total = None
        for n, ref in ((me, own_ref), (me ^ 1, next_ref)):
            hit = (row == s + choose(n, off)) & (s < choose(n, lens))
            t = jnp.dot(jnp.where(hit, 1.0, 0.0).astype(BF16), ref[...], preferred_element_type=F32)
            total = t if total is None else total + t
        if len(outs) > 1:
            outs[i][...] = total.astype(BF16)
        else:
            outs[0][i] = total.astype(BF16)


def packs(cap, count, split, lens, me, own, following):
    u, width = cap // STEPS, own.shape[1]
    if split and count > 1:
        shapes = [jax.ShapeDtypeStruct((u, width), BF16)] * count
    else:
        shapes = [jax.ShapeDtypeStruct((count, u, width), BF16)]
    out = pl.pallas_call(
        functools.partial(pack_kernel, cap),
        in_specs=[pl.BlockSpec(memory_space=pltpu.SMEM)] * 2 + [pl.BlockSpec(memory_space=pltpu.VMEM)] * 2,
        out_specs=[pl.BlockSpec(memory_space=pltpu.VMEM)] * len(shapes),
        out_shape=shapes,
        compiler_params=pltpu.CompilerParams(vmem_limit_bytes=24 * 2**20),
        cost_estimate=pl.CostEstimate(flops=1, bytes_accessed=1, transcendentals=0),
    )(lens, me.reshape(1), own, following)
    return out if split else out[0]


def pieces_kernel(cap, pairs, first, lens_ref, me_ref, *refs):
    parts = refs[:pairs]
    u = cap // STEPS
    lens = [lens_ref[k] for k in range(4)]
    off, al = places(cap, lens)
    if first:
        mine_ref, other_ref, out_ref, wins, held, rows_in = refs[pairs:]
    else:
        wins, _, out_ref, held = refs[pairs:]
    seq = wins.shape[1]
    starts = [off[0], off[1], off[2] + al[2] - seq, off[3] + al[3] - seq]

    if first:

        @pl.when(pl.program_id(0) == 0)
        def _():
            me = me_ref[0]
            c, hc = me % 2, mine_ref.shape[1]
            for p in range(STEPS):
                at = pl.ds(pl.multiple_of(jnp.where(me < 2, p, STEPS - 1 - p) * u, ALIGN), u)
                rows_in[at, pl.ds(pl.multiple_of(c * hc, 128), hc)] = mine_ref[p * u : (p + 1) * u, :]
                rows_in[at, pl.ds(pl.multiple_of((1 - c) * hc, 128), hc)] = other_ref[p * u : (p + 1) * u, :]
            for n in range(4):
                win = rows_in[pl.ds(pl.multiple_of(starts[n], ALIGN), seq), :]
                row = starts[n] + lax.broadcasted_iota(jnp.int32, win.shape, 0)
                valid = (row >= off[n]) & (row < off[n] + lens[n])
                wins[n] = jnp.where(valid, win.astype(F32), 0.0).astype(BF16)

    for j, part in enumerate(parts):
        held[j * u : (j + 1) * u, :] = part[0]
        k = 2 * pairs - 1 - j
        held[k * u : (k + 1) * u, :] = part[1]

    total = None
    for n in range(4):
        at = pl.ds(pl.multiple_of(starts[n], ALIGN), seq)
        proj = lax.dot_general(held[at, :], wins[n], (((0,), (0,)), ((), ())), preferred_element_type=F32)
        total = proj * proj if total is None else total + proj * proj
    out_ref[...] = total.astype(out_ref.dtype)


def squares_of_pieces(cap, lens, me, parts, in_halves, seq, before=None):
    first = before is None
    pairs = len(parts)
    u, cols = parts[0].shape[1:]
    ins = 2 * in_halves[0].shape[1] if first else before[0].shape[1]
    tile = TILE
    per = cols // tile
    side = 0 if first else 1
    at = lambda i, lens, me: ((me[0] % 2 ^ side) * per + i, 0)
    wins = pl.BlockSpec((4, seq, ins), lambda i, lens, me: (0, 0, 0))
    if first:
        more = [pl.BlockSpec((cap, ins // 2), lambda i, lens, me: (0, 0))] * 2
    else:
        more = [wins, pl.BlockSpec(memory_space=pl.ANY)]
        in_halves = [before[1], before[0]]
    result = jax.ShapeDtypeStruct((2 * cols, ins), BF16)
    out = pl.pallas_call(
        functools.partial(pieces_kernel, cap, pairs, first),
        grid_spec=pltpu.PrefetchScalarGridSpec(
            num_scalar_prefetch=2,
            grid=(per,),
            in_specs=[pl.BlockSpec((2, u, tile), lambda i, lens, me: (0, 0, i))] * pairs + more,
            out_specs=[pl.BlockSpec((tile, ins), at)] + ([wins] if first else []),
            scratch_shapes=[pltpu.VMEM((cap, tile), BF16)] + ([pltpu.VMEM((cap, ins), BF16)] if first else []),
        ),
        out_shape=[result] + ([jax.ShapeDtypeStruct((4, seq, ins), BF16)] if first else []),
        input_output_aliases={} if first else {pairs + 3: 0},
        compiler_params=pltpu.CompilerParams(vmem_limit_bytes=36 * 2**20),
        cost_estimate=pl.CostEstimate(flops=1, bytes_accessed=1, transcendentals=0),
    )(lens, me.reshape(1), *parts, *in_halves)
    return out if first else out[0]


def swap_dp(x, k, n_dp):
    return lax.ppermute(x, "dp", [(d, d ^ k) for d in range(n_dp)])


def project_in(kept, blocks, me):
    rows = blocks[0].shape[0]
    total = None
    for k, b in enumerate(blocks):
        a = lax.dynamic_slice_in_dim(kept, (me ^ k) * rows, rows, axis=1)
        t = jnp.dot(a, b, preferred_element_type=F32)
        total = t if total is None else total + t
    return total.astype(BF16)


def mask_acts(acts, lengths):
    keep = (jnp.arange(acts.shape[1], dtype=jnp.int32)[None, :] < lengths[:, None]).astype(acts.dtype)
    return (acts * keep[:, :, None])[0]


def general(n_dp, acts, out_grads, basis_in, basis_out, lengths):
    seq = acts.shape[1]
    me = lax.axis_index("dp")
    kept = mask_acts(acts, lengths)

    def exchange(x, width):
        parts = [lax.dynamic_slice_in_dim(x, (me ^ k) * width, width, axis=1) for k in range(n_dp)]
        return [parts[0]] + [swap_dp(parts[k], k, n_dp) for k in range(1, n_dp)]

    far = swap_dp(basis_in, 2, n_dp)
    blocks = [basis_in, swap_dp(basis_in, 1, n_dp), far, swap_dp(far, 1, n_dp)]
    in_local = project_in(kept, blocks, me)
    n_chunks = 3
    step = seq // n_chunks
    outs = []
    for j in range(n_chunks):
        g = out_grads[0, j * step : (j + 1) * step]
        whole = lax.all_gather(g, "tensor", axis=1, tiled=True)
        mine = jnp.concatenate(exchange(whole, whole.shape[1] // n_dp), axis=0)
        part = jnp.dot(mine, basis_out, preferred_element_type=F32)
        part = part.reshape(n_dp, step, -1)
        odd = swap_dp(part[1::2].astype(BF16), 1, n_dp)
        s0 = part[0] + odd[0].astype(F32)
        s2 = part[2] + odd[1].astype(F32)
        far = swap_dp(jnp.stack([s2, s0]).astype(BF16), 2, n_dp)
        even = jnp.stack([s0 + far[0].astype(F32), s2 + far[1].astype(F32)]).astype(BF16)
        rest = swap_dp(even, 1, n_dp)
        outs.append(jnp.stack([even[0], rest[0], even[1], rest[1]]))
    in_all = lax.all_gather(in_local, "tensor", axis=1, tiled=True)
    in_proj = jnp.stack(exchange(in_all, in_all.shape[1] // n_dp))
    out_proj = jnp.concatenate(outs, axis=1).reshape(n_dp * seq, -1)
    return squares(jnp.arange(n_dp, dtype=jnp.int32) * seq, out_proj, in_proj)


def home_pairs(hops, across=False):
    pairs = []
    for x in (0, 1):
        for c in (0, 1):
            d = 2 * x + c
            for w0, w1 in hops:
                z0, z1 = (w0, w1) if x == 0 else (3 - w0, 3 - w1)
                if across:
                    pairs.append((z0 * 4 + (d ^ 2), z1 * 4 + d))
                else:
                    pairs.append((z0 * 4 + d, z1 * 4 + d))
    return pairs


def send(x, hops, across=False):
    return lax.ppermute(x, ("tensor", "dp"), home_pairs(hops, across))


def to_home(x):
    return send(x, [(0, 0), (1, 1)], True)


def tie(v, *after):
    return lax.optimization_barrier((v,) + after)[0]


def swap(v, k=1):
    return swap_dp(v, k, 4)


def compact(cap, acts, grads, following, basis_in, basis_out, lens):
    seq = acts.shape[1]
    me = lax.axis_index("dp")
    z = lax.axis_index("tensor")
    x, c = me // 2, me % 2
    w = jnp.where(x == 0, z, 3 - z)
    m = STEPS
    u = cap // m
    c2 = min(m, -(-min(2 * seq, cap - 2 * MIN_LEN) // u))
    want_outer = c == x
    kept = mask_acts(acts, lax.dynamic_slice_in_dim(lens, me, 1))

    def pack(a, b, split):
        return packs(cap, c2, split, lens, me, a, b)

    def merged(own, others, i):
        t = None
        if i < c2:
            t = own[i]
        if m - 1 - i < c2:
            o = others[m - 1 - i]
            t = o if t is None else t + o
        return t

    def halves(outer, inner):
        mine = jnp.where(want_outer, outer, inner)
        return mine, swap(jnp.where(want_outer, inner, outer))

    packed = pack(grads, following, True)
    arrived = [None] * c2
    last = None
    for i in range(c2 - 1, -1, -1):
        arrived[i] = to_home(packed[i] if last is None else tie(packed[i], last))
        last = arrived[i]
    far_in = swap(tie(basis_in, last), 2)
    near_in = swap(tie(basis_in, arrived[c2 - 1]))
    far_near = swap(far_in)

    blocks, given, held, sums, fars = ([None] * m for _ in range(5))
    own, fa, fb, m1 = [None] * m, [None] * (m + 1), [None] * m, [None] * m

    def meet(i):
        outer = jnp.where(w == 0, own[i], jnp.where(w == 1, fa[i], jnp.where(w == 2, fb[i], fa[i + 1])))
        inner = jnp.where(w == 0, m1[i], jnp.where(w == 1, own[i], jnp.where(w == 2, fa[i], fb[i])))
        blocks[i] = halves(outer, inner)

    def product(i):
        given[i], held[i] = products(c, *blocks[i], basis_out)

    def add_core(i):
        sums[i] = held[i] + swap(given[i]).astype(F32)
        fars[i] = swap(sums[i].astype(BF16), 2)

    in_local = None
    for i in range(m):
        own[i] = merged(packed, arrived, i)
        v = own[i] if i == 0 else jnp.where(w == 2, fb[i - 1], own[i])
        fa[i] = send(tie(v, *([held[i - 3]] if i >= 3 else [])), [(0, 1), (1, 2)] + ([(2, 3)] if i else []))
        m1[i] = send(own[i], [(1, 0)])
        if i >= 1:
            meet(i - 1)
        if i >= 3:
            add_core(i - 3)
        after = []
        if i >= 2:
            after += blocks[i - 2]
            product(i - 2)
        if i >= 3:
            after.append(sums[i - 3])
        if i == m - 1:
            in_local = project_in(kept, [basis_in, near_in, far_in, far_near], me)
            after.append(in_local)
        fb[i] = send(tie(fa[i], *after), [(1, 2), (2, 3)])

    hc = in_local.shape[1] // 2
    in_mine = lax.dynamic_slice_in_dim(in_local, c * hc, hc, axis=1)
    in_given = lax.dynamic_slice_in_dim(in_local, (1 - c) * hc, hc, axis=1)
    in_packed = pack(in_mine, swap(in_given), False)
    in_arrived = to_home(in_packed)
    in_own = jnp.concatenate([merged(in_packed, in_arrived, i) for i in range(m)], axis=0)

    after = [fb[m - 1], held[m - 3], fars[m - 4], blocks[m - 2][1]]
    fa[m] = send(tie(fb[m - 1], *after), [(2, 3)])
    r1 = send(tie(in_own, *after), [(0, 1), (1, 2)])
    i1 = send(in_own, [(1, 0)])
    add_core(m - 3)
    blocks[m - 2] = (tie(blocks[m - 2][0], fb[m - 1]), blocks[m - 2][1])
    product(m - 2)
    meet(m - 1)
    r2 = send(tie(r1, fa[m], fars[m - 3], held[m - 2]), [(1, 2), (2, 3)])
    add_core(m - 2)
    product(m - 1)
    r3 = send(tie(r2, sums[m - 2], held[m - 1]), [(2, 3)])
    add_core(m - 1)
    outer = jnp.where(w == 0, in_own, jnp.where(w == 1, r1, jnp.where(w == 2, r2, r3)))
    inner = jnp.where(w == 0, i1, jnp.where(w == 1, in_own, jnp.where(w == 2, r1, r2)))
    in_mine, in_other = halves(outer, inner)

    mine, rest = [None] * (m // 2), [None] * (m // 2)
    for j in range(m // 2 - 1, -1, -1):
        k = m - 1 - j
        late = tie(fars[k], in_mine, in_other) if j == 0 else fars[k]
        lo = jnp.where(x == 0, sums[j], sums[k]) + jnp.where(x == 0, late, fars[j]).astype(F32)
        hi = jnp.where(x == 0, sums[k], sums[j]) + jnp.where(x == 0, fars[j], late).astype(F32)
        mine[j] = jnp.stack([lo, hi]).astype(BF16)
        rest[j] = swap(mine[j])

    half = squares_of_pieces(cap, lens, me, mine, [in_mine, in_other], seq)
    return squares_of_pieces(cap, lens, me, rest, None, seq, half)


def special(caps, acts, out_grads, basis_in, basis_out, lengths):
    me = lax.axis_index("dp")
    c = me % 2
    every = lax.all_gather(lengths, ("groups", "dp"), axis=0, tiled=True)
    g = out_grads[0]
    half = g.shape[1] // 2
    mine = lax.dynamic_slice_in_dim(g, c * half, half, axis=1)
    given = lax.dynamic_slice_in_dim(g, (1 - c) * half, half, axis=1)
    following = swap_dp(given, 1, 4)
    totals = jnp.sum(((every + ALIGN - 1) // ALIGN * ALIGN).reshape(-1, 4), axis=1)
    need = jnp.max(totals)
    lens = lax.dynamic_slice_in_dim(every, lax.axis_index("groups") * 4, 4)
    index = jnp.int32(0)
    for cap in caps[:-1]:
        index = index + (need > cap).astype(jnp.int32)
    branches = [functools.partial(compact, cap) for cap in caps]
    return lax.switch(index, branches, acts, mine, following, basis_in, basis_out, lens)


def per_device(sizes, caps, acts, out_grads, basis_in, basis_out, lengths):
    if sizes == (4, 4):
        return special(caps, acts, out_grads, basis_in, basis_out, lengths)
    return general(sizes[1], acts, out_grads, basis_in, basis_out, lengths)


CAPS = (768, 832, 896, 960, 1152)


def solution(mesh):
    in_specs = (
        P(("groups", "dp"), None, None),
        P(("groups", "dp"), None, "tensor"),
        P(("groups", "dp"), "tensor"),
        P(("groups", "dp"), "tensor"),
        P(("groups", "dp")),
    )
    out_specs = P(("groups", "tensor"), "dp")
    sizes = (mesh.shape["tensor"], mesh.shape["dp"])
    return jax.shard_map(
        functools.partial(per_device, sizes, CAPS), mesh=mesh, in_specs=in_specs, out_specs=out_specs, check_vma=False
    )
```

```python
import functools

import jax
import jax.numpy as jnp
from jax import lax
from jax.experimental import pallas as pl
from jax.experimental.pallas import tpu as pltpu
from jax.sharding import PartitionSpec as P

F32 = jnp.float32
BF16 = jnp.bfloat16
MIN_LEN = 96
ALIGN = 16
TILE = 256
STEPS = 4


def square_kernel(start_ref, out_ref, in_ref, c_ref):
    total = None
    for n in range(in_ref.shape[0]):
        rows = pl.ds(pl.multiple_of(start_ref[n], ALIGN), in_ref.shape[1])
        proj = lax.dot_general(out_ref[rows, :], in_ref[n], (((0,), (0,)), ((), ())), preferred_element_type=F32)
        total = proj * proj if total is None else total + proj * proj
    c_ref[...] = total.astype(c_ref.dtype)


def squares(starts, out_proj, in_proj):
    tokens, cols = out_proj.shape
    n, seq, ins = in_proj.shape
    tile = cols
    for t in (512, 256, 128):
        if cols % t == 0:
            tile = t
            break
    return pl.pallas_call(
        square_kernel,
        grid_spec=pltpu.PrefetchScalarGridSpec(
            num_scalar_prefetch=1,
            grid=(cols // tile,),
            in_specs=[
                pl.BlockSpec((tokens, tile), lambda i, s: (0, i)),
                pl.BlockSpec((n, seq, ins), lambda i, s: (0, 0, 0)),
            ],
            out_specs=pl.BlockSpec((tile, ins), lambda i, s: (i, 0)),
        ),
        out_shape=jax.ShapeDtypeStruct((cols, ins), BF16),
        compiler_params=pltpu.CompilerParams(vmem_limit_bytes=60 * 2**20),
        cost_estimate=pl.CostEstimate(
            flops=2 * n * seq * cols * ins, bytes_accessed=2 * (n * seq * (cols + ins) + cols * ins), transcendentals=0
        ),
    )(starts, out_proj, in_proj)


def product_kernel(c_ref, mine_ref, other_ref, b_mine_ref, b_other_ref, given_ref, held_ref):
    i = pl.program_id(0)
    total = jnp.dot(mine_ref[...], b_mine_ref[...], preferred_element_type=F32)
    total = total + jnp.dot(other_ref[...], b_other_ref[...], preferred_element_type=F32)

    @pl.when(i < pl.num_programs(0) // 2)
    def _():
        given_ref[...] = total.astype(given_ref.dtype)

    @pl.when(i >= pl.num_programs(0) // 2)
    def _():
        held_ref[...] = total


def products(c, mine, other, basis):
    rows, depth = mine.shape
    cols = basis.shape[1] // 2
    tile = 896 if cols % 896 == 0 else TILE
    per = cols // tile
    at = lambda i, c: jnp.where(i < per, (1 - c[0]) * per + i, c[0] * per + i - per)
    return pl.pallas_call(
        product_kernel,
        grid_spec=pltpu.PrefetchScalarGridSpec(
            num_scalar_prefetch=1,
            grid=(2 * per,),
            in_specs=[
                pl.BlockSpec((rows, depth), lambda i, c: (0, 0)),
                pl.BlockSpec((rows, depth), lambda i, c: (0, 0)),
                pl.BlockSpec((depth, tile), lambda i, c: (c[0], at(i, c))),
                pl.BlockSpec((depth, tile), lambda i, c: (1 - c[0], at(i, c))),
            ],
            out_specs=[
                pl.BlockSpec((rows, tile), lambda i, c: (0, jnp.minimum(i, per - 1))),
                pl.BlockSpec((rows, tile), lambda i, c: (0, jnp.maximum(i - per, 0))),
            ],
        ),
        out_shape=[jax.ShapeDtypeStruct((rows, cols), BF16), jax.ShapeDtypeStruct((rows, cols), F32)],
        compiler_params=pltpu.CompilerParams(vmem_limit_bytes=36 * 2**20),
        cost_estimate=pl.CostEstimate(flops=1, bytes_accessed=1, transcendentals=0),
    )(c.reshape(1), mine, other, basis, basis)


def pieces_kernel(pairs, start_ref, c_ref, *refs):
    own, rest, in_ref, out_ref, held = refs[:pairs], refs[pairs : 2 * pairs], refs[-3], refs[-2], refs[-1]
    i = pl.program_id(0)
    u = own[0].shape[1]

    def fill(parts):
        for j, part in enumerate(parts):
            held[j * u : (j + 1) * u, :] = part[0]
            k = 2 * pairs - 1 - j
            held[k * u : (k + 1) * u, :] = part[1]

    @pl.when(i < pl.num_programs(0) // 2)
    def _():
        fill(own)

    @pl.when(i >= pl.num_programs(0) // 2)
    def _():
        fill(rest)

    total = None
    for n in range(in_ref.shape[0]):
        rows = pl.ds(pl.multiple_of(start_ref[n], ALIGN), in_ref.shape[1])
        proj = lax.dot_general(held[rows, :], in_ref[n], (((0,), (0,)), ((), ())), preferred_element_type=F32)
        total = proj * proj if total is None else total + proj * proj
    out_ref[...] = total.astype(out_ref.dtype)


def squares_of_pieces(starts, c, own, rest, wins):
    pairs = len(own)
    u, cols = own[0].shape[1:]
    n, seq, ins = wins.shape
    tile = 896 if cols % 896 == 0 else TILE
    per = cols // tile
    at = lambda i, s, c: (jnp.where(i < per, c[0] * per + i, (1 - c[0]) * per + i - per), 0)
    return pl.pallas_call(
        functools.partial(pieces_kernel, pairs),
        grid_spec=pltpu.PrefetchScalarGridSpec(
            num_scalar_prefetch=2,
            grid=(2 * per,),
            in_specs=[pl.BlockSpec((2, u, tile), lambda i, s, c: (0, 0, jnp.minimum(i, per - 1)))] * pairs
            + [pl.BlockSpec((2, u, tile), lambda i, s, c: (0, 0, jnp.maximum(i - per, 0)))] * pairs
            + [pl.BlockSpec((n, seq, ins), lambda i, s, c: (0, 0, 0))],
            out_specs=pl.BlockSpec((tile, ins), at),
            scratch_shapes=[pltpu.VMEM((2 * pairs * u, tile), BF16)],
        ),
        out_shape=jax.ShapeDtypeStruct((2 * cols, ins), BF16),
        compiler_params=pltpu.CompilerParams(vmem_limit_bytes=40 * 2**20),
        cost_estimate=pl.CostEstimate(flops=1, bytes_accessed=1, transcendentals=0),
    )(starts, c.reshape(1), *own, *rest, wins)


def swap_dp(x, k, n_dp):
    return lax.ppermute(x, "dp", [(d, d ^ k) for d in range(n_dp)])


def project_in(kept, blocks, me):
    rows = blocks[0].shape[0]
    total = None
    for k, b in enumerate(blocks):
        a = lax.dynamic_slice_in_dim(kept, (me ^ k) * rows, rows, axis=1)
        t = jnp.dot(a, b, preferred_element_type=F32)
        total = t if total is None else total + t
    return total.astype(BF16)


def mask_acts(acts, lengths):
    keep = (jnp.arange(acts.shape[1], dtype=jnp.int32)[None, :] < lengths[:, None]).astype(acts.dtype)
    return (acts * keep[:, :, None])[0]


def general(n_dp, acts, out_grads, basis_in, basis_out, lengths):
    seq = acts.shape[1]
    me = lax.axis_index("dp")
    kept = mask_acts(acts, lengths)

    def exchange(x, width):
        parts = [lax.dynamic_slice_in_dim(x, (me ^ k) * width, width, axis=1) for k in range(n_dp)]
        return [parts[0]] + [swap_dp(parts[k], k, n_dp) for k in range(1, n_dp)]

    far = swap_dp(basis_in, 2, n_dp)
    blocks = [basis_in, swap_dp(basis_in, 1, n_dp), far, swap_dp(far, 1, n_dp)]
    in_local = project_in(kept, blocks, me)
    n_chunks = 3
    step = seq // n_chunks
    outs = []
    for j in range(n_chunks):
        g = out_grads[0, j * step : (j + 1) * step]
        whole = lax.all_gather(g, "tensor", axis=1, tiled=True)
        mine = jnp.concatenate(exchange(whole, whole.shape[1] // n_dp), axis=0)
        part = jnp.dot(mine, basis_out, preferred_element_type=F32)
        part = part.reshape(n_dp, step, -1)
        odd = swap_dp(part[1::2].astype(BF16), 1, n_dp)
        s0 = part[0] + odd[0].astype(F32)
        s2 = part[2] + odd[1].astype(F32)
        far = swap_dp(jnp.stack([s2, s0]).astype(BF16), 2, n_dp)
        even = jnp.stack([s0 + far[0].astype(F32), s2 + far[1].astype(F32)]).astype(BF16)
        rest = swap_dp(even, 1, n_dp)
        outs.append(jnp.stack([even[0], rest[0], even[1], rest[1]]))
    in_all = lax.all_gather(in_local, "tensor", axis=1, tiled=True)
    in_proj = jnp.stack(exchange(in_all, in_all.shape[1] // n_dp))
    out_proj = jnp.concatenate(outs, axis=1).reshape(n_dp * seq, -1)
    return squares(jnp.arange(n_dp, dtype=jnp.int32) * seq, out_proj, in_proj)


def home_pairs(hops, across=False):
    pairs = []
    for x in (0, 1):
        for c in (0, 1):
            d = 2 * x + c
            for w0, w1 in hops:
                z0, z1 = (w0, w1) if x == 0 else (3 - w0, 3 - w1)
                if across:
                    pairs.append((z0 * 4 + (d ^ 2), z1 * 4 + d))
                else:
                    pairs.append((z0 * 4 + d, z1 * 4 + d))
    return pairs


def send(x, hops, across=False):
    return lax.ppermute(x, ("tensor", "dp"), home_pairs(hops, across))


def to_home(x):
    return send(x, [(0, 0), (1, 1)], True)


def tie(v, *after):
    return lax.optimization_barrier((v,) + after)[0]


def swap(v, k=1):
    return swap_dp(v, k, 4)


def compact(cap, acts, grads, basis_in, basis_out, lens):
    seq = acts.shape[1]
    me = lax.axis_index("dp")
    z = lax.axis_index("tensor")
    x, c = me // 2, me % 2
    w = jnp.where(x == 0, z, 3 - z)
    m = STEPS
    u = cap // m
    c2 = min(m, -(-min(2 * seq, cap - 2 * MIN_LEN) // u))
    want_outer = c == x
    kept = mask_acts(acts, lax.dynamic_slice_in_dim(lens, me, 1))

    al = (lens + ALIGN - 1) // ALIGN * ALIGN
    off = jnp.stack([jnp.int32(0), al[0], cap - al[3] - al[2], cap - al[3]])

    pos = jnp.arange(c2 * u, dtype=jnp.int32)
    chunk = pos // u
    row = jnp.where(x == 0, chunk, m - 1 - chunk) * u + pos % u
    s = jnp.arange(seq, dtype=jnp.int32)

    def pick(n):
        return (row[:, None] == (off[n] + s)[None, :]) & (s < lens[n])[None, :]

    hot = jnp.concatenate([pick(me), pick(me ^ 1)], axis=1).astype(BF16)

    def pack(v):
        return jnp.dot(hot, v, preferred_element_type=F32).astype(BF16).reshape(c2, u, v.shape[1])

    def merged(own, others, i):
        t = None
        if i < c2:
            t = own[i]
        if m - 1 - i < c2:
            o = others[m - 1 - i]
            t = o if t is None else t + o
        return t

    def halves(outer, inner):
        mine = jnp.where(want_outer, outer, inner)
        return mine, swap(jnp.where(want_outer, inner, outer))

    packed = pack(grads)
    arrived = [None] * c2
    last = None
    for i in range(c2 - 1, -1, -1):
        arrived[i] = to_home(packed[i] if last is None else tie(packed[i], last))
        last = arrived[i]
    far_in = swap(tie(basis_in, last), 2)
    near_in = swap(tie(basis_in, arrived[c2 - 1]))
    far_near = swap(far_in)

    blocks, given, held, sums, fars = ([None] * m for _ in range(5))
    own, fa, fb, m1 = [None] * m, [None] * (m + 1), [None] * m, [None] * m

    def meet(i):
        outer = jnp.where(w == 0, own[i], jnp.where(w == 1, fa[i], jnp.where(w == 2, fb[i], fa[i + 1])))
        inner = jnp.where(w == 0, m1[i], jnp.where(w == 1, own[i], jnp.where(w == 2, fa[i], fb[i])))
        blocks[i] = halves(outer, inner)

    def product(i):
        given[i], held[i] = products(c, *blocks[i], basis_out)

    def add_core(i):
        sums[i] = held[i] + swap(given[i]).astype(F32)
        fars[i] = swap(sums[i].astype(BF16), 2)

    in_local = None
    for i in range(m):
        own[i] = merged(packed, arrived, i)
        v = own[i] if i == 0 else jnp.where(w == 2, fb[i - 1], own[i])
        fa[i] = send(tie(v, *([held[i - 3]] if i >= 3 else [])), [(0, 1), (1, 2)] + ([(2, 3)] if i else []))
        m1[i] = send(own[i], [(1, 0)])
        if i >= 1:
            meet(i - 1)
        if i >= 3:
            add_core(i - 3)
        after = []
        if i >= 2:
            after += blocks[i - 2]
            product(i - 2)
        if i >= 3:
            after.append(sums[i - 3])
        if i == m - 1:
            in_local = project_in(kept, [basis_in, near_in, far_in, far_near], me)
            after.append(in_local)
        fb[i] = send(tie(fa[i], *after), [(1, 2), (2, 3)])

    hc = in_local.shape[1] // 2
    in_mine = lax.dynamic_slice_in_dim(in_local, c * hc, hc, axis=1)
    in_given = lax.dynamic_slice_in_dim(in_local, (1 - c) * hc, hc, axis=1)
    in_packed = pack(jnp.concatenate([in_mine, swap(in_given)], axis=0))
    in_arrived = to_home(in_packed)
    in_own = jnp.concatenate([merged(in_packed, in_arrived, i) for i in range(m)], axis=0)

    after = [fb[m - 1], held[m - 3], fars[m - 4], blocks[m - 2][1]]
    fa[m] = send(tie(fb[m - 1], *after), [(2, 3)])
    r1 = send(tie(in_own, *after), [(0, 1), (1, 2)])
    i1 = send(in_own, [(1, 0)])
    add_core(m - 3)
    blocks[m - 2] = (tie(blocks[m - 2][0], fb[m - 1]), blocks[m - 2][1])
    product(m - 2)
    meet(m - 1)
    r2 = send(tie(r1, fa[m], fars[m - 3], held[m - 2]), [(1, 2), (2, 3)])
    add_core(m - 2)
    product(m - 1)
    r3 = send(tie(r2, sums[m - 2], held[m - 1]), [(2, 3)])
    add_core(m - 1)
    outer = jnp.where(w == 0, in_own, jnp.where(w == 1, r1, jnp.where(w == 2, r2, r3)))
    inner = jnp.where(w == 0, i1, jnp.where(w == 1, in_own, jnp.where(w == 2, r1, r2)))
    mine, other = halves(outer, inner)
    in_t = jnp.where(c == 0, jnp.concatenate([mine, other], 1), jnp.concatenate([other, mine], 1))
    in_t = in_t.reshape(m, u, 2 * hc)
    in_t = jnp.where(x == 0, in_t, in_t[::-1]).reshape(cap, 2 * hc)

    mine, rest = [None] * (m // 2), [None] * (m // 2)
    for j in range(m // 2 - 1, -1, -1):
        k = m - 1 - j
        lo = jnp.where(x == 0, sums[j], sums[k]) + jnp.where(x == 0, fars[k], fars[j]).astype(F32)
        hi = jnp.where(x == 0, sums[k], sums[j]) + jnp.where(x == 0, fars[j], fars[k]).astype(F32)
        mine[j] = jnp.stack([lo, hi]).astype(BF16)
        rest[j] = swap(mine[j])

    ends = off + al
    starts = jnp.stack([off[0], off[1], ends[2] - seq, ends[3] - seq]).astype(jnp.int32)
    wins = []
    for n in range(4):
        rows = starts[n] + s
        valid = (rows >= off[n]) & (rows < off[n] + lens[n])
        win = lax.dynamic_slice_in_dim(in_t, starts[n], seq, axis=0)
        wins.append(jnp.where(valid[:, None], win, jnp.zeros_like(win)))
    return squares_of_pieces(starts, c, mine, rest, jnp.stack(wins))


def special(caps, acts, out_grads, basis_in, basis_out, lengths):
    me = lax.axis_index("dp")
    c = me % 2
    every = lax.all_gather(lengths, ("groups", "dp"), axis=0, tiled=True)
    g = out_grads[0]
    half = g.shape[1] // 2
    mine = lax.dynamic_slice_in_dim(g, c * half, half, axis=1)
    given = lax.dynamic_slice_in_dim(g, (1 - c) * half, half, axis=1)
    grads = jnp.concatenate([mine, swap_dp(given, 1, 4)], axis=0)
    totals = jnp.sum(((every + ALIGN - 1) // ALIGN * ALIGN).reshape(-1, 4), axis=1)
    need = jnp.max(totals)
    lens = lax.dynamic_slice_in_dim(every, lax.axis_index("groups") * 4, 4)
    index = jnp.int32(0)
    for cap in caps[:-1]:
        index = index + (need > cap).astype(jnp.int32)
    branches = [functools.partial(compact, cap) for cap in caps]
    return lax.switch(index, branches, acts, grads, basis_in, basis_out, lens)


def per_device(sizes, caps, acts, out_grads, basis_in, basis_out, lengths):
    if sizes == (4, 4):
        return special(caps, acts, out_grads, basis_in, basis_out, lengths)
    return general(sizes[1], acts, out_grads, basis_in, basis_out, lengths)


CAPS = (768, 832, 896, 960, 1152)


def solution(mesh):
    in_specs = (
        P(("groups", "dp"), None, None),
        P(("groups", "dp"), None, "tensor"),
        P(("groups", "dp"), "tensor"),
        P(("groups", "dp"), "tensor"),
        P(("groups", "dp")),
    )
    out_specs = P(("groups", "tensor"), "dp")
    sizes = (mesh.shape["tensor"], mesh.shape["dp"])
    return jax.shard_map(
        functools.partial(per_device, sizes, CAPS), mesh=mesh, in_specs=in_specs, out_specs=out_specs, check_vma=False
    )
```
